512 devices in a mesh: rows: 32 (over y_hi, z), cols: 16 (over y_lo, x, core).
Axes of the slice: x: 4, y: 4 (y_hi: 2, y_lo: 2; y = y_hi * 2 + y_lo), z: 16, core: 2. Of those that a mesh axis runs over, the one named last changes fastest.
Arguments:
- features: float32 [16384, 512], P('rows', 'cols'), may hold values from -6 to 6
- weight: float32 [512, 512], replicated, may hold values from -0.25 to 0.25
- tile_cols: int32 [128, 12], P('rows'), may hold values from 0 to 127
- tile_count: int32 [128], P('rows'), may hold values from 1 to 12, as said below
- tile_values: float32 [128, 12, 128, 128], P('rows'), may hold values from -0.5 to 0.5
- cotangent: float32 [16384, 512], P('rows', 'cols'), may hold values from -6 to 6
Outputs:
- activated: float32 [16384, 512], P('rows', 'cols')
- grad_features: float32 [16384, 512], P('rows', 'cols')
- grad_weight: float32 [512, 512], P('cols', 'rows')
The draws below stay inside these ranges and needn't reach their ends.
Inputs may be any that keep to these rules, and one draw needn't show every extreme that they name: Tile row r uses the slots 0 to tile_count[r] - 1; the entries of later slots are ignored. Some tile row uses all 12 slots. `tile_cols`: A tile column may repeat within a tile row.
All inputs are finite; a program needn't handle non-finite values.
Results may differ from the reference program's by a relative error of at most 0.0001.
Values sent between devices are 32-bit elements; how exact they have to be, the bound alone decides.
No kernel may reach another device: no remote copies, remote signals or barrier semaphores. Data moves between devices by JAX's collectives and lax.ppermute only.
A program may use at most 64 MiB of HBM per device.

```python
import jax
import jax.numpy as jnp
from jax import lax

F = 512
TILE = 128
KMAX = 12
RB = 512
NODES = 16384
NT = 128


def draw_tile_count(key, part):
    key = jax.random.fold_in(key, 11)
    first_key, second_key = jax.random.split(key)
    per_block = RB // TILE
    levels = jax.random.randint(first_key, (NT // per_block,), 0, 3)
    spread_levels = jnp.repeat(levels, per_block)
    base = jax.random.randint(second_key, (NT,), 0, KMAX)
    counted = 1 + base * (spread_levels + 1) // 3
    counted = counted.at[0].set(KMAX)
    return counted.astype(jnp.int32)


def plant(result, rng, smallest, high):
    dims = result.shape
    index_at = [jax.random.randint(jax.random.fold_in(rng, axis), (), 0, dims[axis]) for axis in range(len(dims))]
    result = result.at[tuple(index_at)].set(smallest)
    longest = dims.index(max(dims))
    index_at[longest] = (index_at[longest] + 1) % dims[longest]
    return result.at[tuple(index_at)].set(high)


def block_levels(own_key, dims, cuts, smallest, largest):
    def one(dim, blocks):
        heights = jax.random.uniform(jax.random.fold_in(jax.random.fold_in(own_key, 6), dim), (blocks,), jnp.float32, smallest / len(cuts), largest / len(cuts))
        return jnp.repeat(jnp.exp(heights), dims[dim] // blocks).reshape((-1,) + (1,) * (len(dims) - dim - 1))

    level = one(*cuts[0])
    for cut in cuts[1:]:
        level = level * one(*cut)
    return level


def centred(key, shape, scale, limit, shards=(), held_as=jnp.bfloat16):
    level = block_levels(key, shape, shards, -0.22, 0.18) if shards else 1.0
    values = jax.random.normal(key, shape, jnp.float32) * scale * level
    return jnp.minimum(jnp.maximum(values, -limit), limit).astype(held_as)


def setup_inputs(seed: int = 0) -> dict:
    splits = jax.random.split(jax.random.key(seed), 7)
    return {
        "features": centred(splits[0], (NODES, F), 1.0, 6.0, ((0, 32), (1, 16)), jnp.float32),
        "weight": centred(splits[1], (F, F), F ** -0.5, 0.25, (), jnp.float32),
        "tile_cols": plant(jax.random.randint(splits[2], (NT, KMAX), 0, NT), jax.random.fold_in(splits[2], 1), 0, NT - 1).astype(jnp.int32),
        "tile_count": draw_tile_count(jax.random.fold_in(splits[6], 71), 0),
        "tile_values": centred(splits[4], (NT, KMAX, TILE, TILE), TILE ** -0.5, 0.5, ((0, 32),), jnp.float32),
        "cotangent": centred(splits[5], (NODES, F), 1.0, 6.0, ((0, 32), (1, 16)), jnp.float32),
    }


def tile_scales(tile_count):
    slot_ids = jnp.arange(KMAX)
    filled = jnp.where(slot_ids[None, :] < tile_count[:, None], 1.0, 0.0).astype(jnp.float32)
    return filled / jnp.sqrt(tile_count.astype(jnp.float32))[:, None]

def aggregate(values, tile_cols, scales, tile_values):
    blocks = values.reshape(NT, TILE, F)

    def per_row(inputs):
        columns, factors, tiles = inputs
        picked = blocks[columns]
        return jnp.einsum('sab,sbf->af', tiles * factors[:, None, None], picked, precision=lax.Precision.HIGHEST)
    summed = lax.map(per_row, (tile_cols, scales, tile_values))
    return summed.reshape(NODES, F)

def spread(gradient, tile_cols, scales, tile_values):
    grad_blocks = gradient.reshape(NT, TILE, F)

    def add_row(summed, inputs):
        columns, factors, tiles, grad_block = inputs
        contrib = jnp.einsum('sab,af->sbf', tiles * factors[:, None, None], grad_block, precision=lax.Precision.HIGHEST)
        return (summed.at[columns].add(contrib), None)
    summed, _ = lax.scan(add_row, jnp.zeros((NT, TILE, F), jnp.float32), (tile_cols, scales, tile_values, grad_blocks))
    return summed.reshape(NODES, F)

def reference(features, weight, tile_cols, tile_count, tile_values, cotangent):
    scales = tile_scales(tile_count)
    aggregated = aggregate(features, tile_cols, scales, tile_values)
    preact = jnp.dot(aggregated, weight, precision=lax.Precision.HIGHEST)
    sigmoid_pre = jax.nn.sigmoid(preact)
    activated = preact * sigmoid_pre
    grad_pre = cotangent * (sigmoid_pre + preact * sigmoid_pre * (1.0 - sigmoid_pre))
    grad_weight = jnp.dot(aggregated.T, grad_pre, precision=lax.Precision.HIGHEST)
    grad_agg = jnp.dot(grad_pre, weight.T, precision=lax.Precision.HIGHEST)
    grad_features = spread(grad_agg, tile_cols, scales, tile_values)
    return (activated, grad_features, grad_weight)
```

```python
import jax
import jax.numpy as jnp
from jax import lax
from jax.experimental import pallas as pl
from jax.experimental.pallas import tpu as pltpu
from jax.sharding import Mesh, PartitionSpec as P

ROWS = ("yh", "zh", "zl")
RING = ("zh", "zl")
COLS = ("yl", "x", "core")
F = 512
W = 32
T = 128
K = 12
TR = 4
C = 16
G = 4
BLK = TR * W + 8
f32, bf16 = jnp.float32, jnp.bfloat16
VMEM = pl.BlockSpec(memory_space=pltpu.VMEM)
SMEM = pl.BlockSpec(memory_space=pltpu.SMEM)
NT_DIMS = (((1,), (1,)), ((), ()))
NN_DIMS = (((1,), (0,)), ((), ()))
TN_DIMS = (((0,), (0,)), ((), ()))


def dot(a, b, dims=NN_DIMS):
    return lax.dot_general(a, b, dims, preferred_element_type=f32)


def split(x):
    hi = x.astype(bf16)
    return hi, (x - hi.astype(f32)).astype(bf16)


def call(kernel, outs, flops, moved, scratch=(), specs=None):
    return pl.pallas_call(
        kernel,
        out_shape=outs,
        in_specs=specs,
        out_specs=jax.tree.map(lambda _: VMEM, outs),
        scratch_shapes=scratch,
        compiler_params=pltpu.CompilerParams(vmem_limit_bytes=40 * 2**20),
        cost_estimate=pl.CostEstimate(flops=flops, bytes_accessed=moved, transcendentals=0),
    )


def scaled_tiles(scale_ref, tiles_ref, t):
    parts = [split(tiles_ref[t, s] * scale_ref[t, s]) for s in range(K)]
    return jnp.concatenate([p[0] for p in parts], 1), jnp.concatenate([p[1] for p in parts], 1)


def regroup(piece):
    return [jnp.concatenate([piece(g, k) for g in range(G)], 1) for k in range(4)]


def weight_kernel(w_ref, out_ref):
    rows = [w_ref[c * W + g * 8:c * W + g * 8 + 8, :] for g in range(G) for c in range(C)]
    hi, lo = split(jnp.concatenate(rows, 0))
    old = lax.broadcasted_iota(jnp.int32, (F, F), 0)
    new = lax.broadcasted_iota(jnp.int32, (F, F), 1)
    source = ((new // 8) % C) * W + (new // (8 * C)) * 8 + new % 8
    order = jnp.where(old == source, 1.0, 0.0).astype(bf16)
    out_ref[0] = dot(hi, order).astype(bf16)
    out_ref[1] = dot(lo, order).astype(bf16)


def gather_kernel(cols_ref, scale_ref, pos_ref, own_ref, a_ref, b_ref, c_ref, d_ref, tiles_ref, cot_ref, out_ref, held):
    def keep(ref, at, y):
        hi, lo = split(ref[...].reshape(16, W, T) if y is None else ref[y].reshape(16, W, T))
        held[at:at + 16, 0:W] = hi
        held[at:at + 16, W:2 * W] = lo

    for y in range(2):
        keep(own_ref, y * 16, y)
        keep(b_ref, 32 + y * 16, y)
        keep(a_ref, 96 + y * 16, y)
    keep(c_ref, 64, None)
    keep(d_ref, 80, None)
    yh, zl = pos_ref[0], pos_ref[1]
    for t in range(TR):
        picked = []
        for s in range(K):
            col = cols_ref[t, s]
            rel_q = ((col // 4) % 4 - zl + 4) % 4
            rel_y = (col // 64 - yh + 2) % 2
            picked.append(held[rel_q * 32 + rel_y * 16 + ((col // 16) % 4) * 4 + col % 4])
        left = jnp.concatenate(picked, 1)
        hi, lo = scaled_tiles(scale_ref, tiles_ref, t)
        both = dot(left, hi, NT_DIMS)
        agg = both[:W] + both[W:] + dot(left[:W], lo, NT_DIMS)
        parts = regroup(lambda g, k: agg[8 * g:8 * g + 8, W * k:W * k + W])
        cots = regroup(lambda g, k: cot_ref[8 * g:8 * g + 8, T * t + W * k:T * t + W * k + W])
        for k in range(4):
            out_ref[4 * t + k, 0:8, :] = parts[k]
            out_ref[4 * t + k, 8:16, :] = cots[k]


def node_rows(block):
    turned = block.reshape(T, T).T
    return jnp.concatenate([turned[W * g:W * g + W] for g in range(G)], 1)


def node_cols(rows):
    turned = jnp.concatenate([rows[:, T * g:T * g + T] for g in range(G)], 0)
    return turned.T.reshape(C, 8, T)


def layer_kernel(in_ref, w_ref, out_ref):
    agg = node_rows(in_ref[:, 0:8, :])
    cot = node_rows(in_ref[:, 8:16, :])
    agg_hi, agg_lo = split(agg)
    both = dot(jnp.concatenate([agg_hi, agg_lo], 0), w_ref[0])
    pre = both[:W] + both[W:] + dot(agg_hi, w_ref[1])
    sig = jax.nn.sigmoid(pre)
    act = pre * sig
    grad = cot * (sig + act * (1.0 - sig))
    grad_hi, grad_lo = split(grad)
    both = dot(jnp.concatenate([grad_hi, grad_lo], 0), w_ref[0], NT_DIMS)
    back = both[:W] + both[W:] + dot(grad_hi, w_ref[1], NT_DIMS)
    out_ref[:, 0:8, :] = node_cols(back)
    out_ref[:, 8:16, :] = node_cols(act)
    left = jnp.concatenate([agg_hi, agg_lo, agg_hi], 0)
    right = jnp.concatenate([grad_hi, grad_hi, grad_lo], 0)
    for g in range(G):
        part = dot(left[:, T * g:T * g + T], right, TN_DIMS)
        for h in range(4):
            at = 16 + (4 * g + h) * 8
            out_ref[:, at:at + 8, :] = part[:, T * h:T * h + T].reshape(C, 8, T)


def spread_kernel(cols_ref, scale_ref, pos_ref, in_ref, tiles_ref, act_ref, out_ref, weight_part):
    yh, zl = pos_ref[0], pos_ref[1]
    total = in_ref[0, 16:16 + T, :]
    for c in range(1, C):
        total = total + in_ref[c, 16:16 + T, :]
    weight_part[...] = total.T
    out_ref[:, 0:TR * W, :] = jnp.zeros((32, TR * W, T), f32)
    for q in range(4):
        for y in range(2):
            for m in range(4):
                block = ((yh + y) % 2) * 16 + m * 4 + (zl + q) % 4
                start = pl.multiple_of((block // 2) * 8, 8)
                out_ref[q * 8 + y * 4 + m, TR * W:BLK, :] = weight_part[pl.ds(start, 8), :]
    for t in range(TR):
        grad = regroup(lambda k, g: in_ref[4 * t + k, 0:8, W * g:W * g + W])
        act = regroup(lambda k, g: in_ref[4 * t + k, 8:16, W * g:W * g + W])
        act_ref[:, T * t:T * t + T] = jnp.concatenate(act, 0)
        grad_hi, grad_lo = split(jnp.concatenate(grad, 0))
        hi, lo = scaled_tiles(scale_ref, tiles_ref, t)
        both = dot(jnp.concatenate([grad_hi, grad_lo], 0), hi)
        sent = both[:W] + both[W:] + dot(grad_hi, lo)
        for s in range(K):
            col = cols_ref[t, s]
            rel_q = ((col // 4) % 4 - zl + 4) % 4
            rel_y = (col // 64 - yh + 2) % 2
            block = rel_q * 8 + rel_y * 4 + (col // 16) % 4
            at = pl.ds(pl.multiple_of((col % 4) * W, W), W)
            out_ref[block, at, :] = out_ref[block, at, :] + sent[:, T * s:T * s + T]


def last_kernel(pos_ref, in_ref, grad_ref, weight_ref):
    total = in_ref[0] + in_ref[1] + in_ref[2] + in_ref[3]
    for t in range(TR):
        grad_ref[:, T * t:T * t + T] = total[W * t:W * t + W]
    piece = total[TR * W:BLK]
    odd = jnp.concatenate([piece[:, 16:], piece[:, :16]], 1)
    piece = jnp.where(pos_ref[1] % 2 == 1, odd, piece)
    for h in range(2):
        cut = [piece[:, W * g + 8 * h:W * g + 8 * h + 8] for g in range(G)]
        weight_ref[8 * h:8 * h + 8, :] = jnp.concatenate(cut, 1)


def shift(size, by):
    return [(i, (i + by) % size) for i in range(size)]


def local(features, weight, tile_cols, tile_count, tile_values, cotangent):
    counts = tile_count.astype(f32)
    slots = lax.broadcasted_iota(jnp.int32, (TR, K), 1)
    scales = jnp.where(slots < tile_count[:, None], 1.0, 0.0) / jnp.sqrt(counts)[:, None]
    pos = jnp.stack([lax.axis_index("yh"), lax.axis_index("zl")]).astype(jnp.int32)
    shape = jax.ShapeDtypeStruct

    with jax.named_scope("gather_features"):
        mine = features.T.reshape(W, TR, T).transpose(1, 0, 2)
        far = lax.all_gather(mine, "zh")
        own = jnp.stack([far, lax.ppermute(far, "yh", shift(2, 1))])
        a = lax.ppermute(own, RING, shift(16, 1))
        b = lax.ppermute(own, RING, shift(16, -1))
        c = lax.ppermute(own[0], RING, shift(16, 2))
        d = lax.ppermute(own[1], RING, shift(16, -2))
    weight_parts = call(weight_kernel, shape((2, F, F), bf16), 4 * F**3, 2**21, specs=[VMEM])(weight)
    packed = call(
        gather_kernel, shape((C, 16, T), f32), 10**8, 6 * 2**20, [pltpu.VMEM((128, 2 * W, T), bf16)],
        specs=[SMEM] * 3 + [VMEM] * 7,
    )(tile_cols, scales, pos, own, a, b, c, d, tile_values, cotangent.T)
    with jax.named_scope("to_nodes"):
        packed = lax.all_to_all(packed, COLS, 0, 0)
    layer = call(layer_kernel, shape((C, 16 + T, T), f32), 10**8, 3 * 2**20, specs=[VMEM] * 2)(packed, weight_parts)
    with jax.named_scope("to_features"):
        layer = lax.all_to_all(layer, COLS, 0, 0)
    activated, parts = call(
        spread_kernel, (shape((W, TR * T), f32), shape((32, BLK, T), f32)), 10**8, 7 * 2**20,
        [pltpu.VMEM((T, T), f32)], specs=[SMEM] * 3 + [VMEM] * 2,
    )(tile_cols, scales, pos, layer, tile_values)
    with jax.named_scope("add_blocks"):
        parts = parts.reshape(4, 2, 4, BLK, T)
        a = lax.ppermute(parts[1], RING, shift(16, 1))
        b = lax.ppermute(parts[3], RING, shift(16, -1))
        c = lax.ppermute(parts[2, 0], RING, shift(16, 2))
        d = lax.ppermute(parts[2, 1], RING, shift(16, -2))
        other = parts[0, 1] + a[1] + b[1] + d
        same = parts[0, 0] + a[0] + b[0] + c
        same = same + lax.ppermute(other, "yh", shift(2, 1))
        same = lax.all_to_all(same, "zh", 0, 0)
    grad_features, grad_weight = call(
        last_kernel, (shape((W, TR * T), f32), shape((16, W), f32)), 10**6, 2**19, specs=[SMEM, VMEM],
    )(pos, same)
    return activated.T, grad_features.T, grad_weight.T


def solution(mesh):
    grid = Mesh(mesh.devices.reshape(2, 4, 4, 2, 4, 2), ROWS + COLS)
    return jax.shard_map(
        local,
        mesh=grid,
        in_specs=(P(ROWS, COLS), P(), P(ROWS, None), P(ROWS), P(ROWS, None, None, None), P(ROWS, COLS)),
        out_specs=(P(ROWS, COLS), P(ROWS, COLS), P(COLS, ROWS)),
        check_vma=False,
    )
```

```python
import jax
import jax.numpy as jnp
from jax import lax
from jax.experimental import pallas as pl
from jax.experimental.pallas import tpu as pltpu
from jax.sharding import Mesh, PartitionSpec as P

ROWS = ("yh", "zh", "zl")
RING = ("zh", "zl")
COLS = ("yl", "x", "core")
F = 512
W = 32
T = 128
K = 12
TR = 4
C = 16
G = 4
BLK = TR * W + 8
f32, bf16 = jnp.float32, jnp.bfloat16
VMEM = pl.BlockSpec(memory_space=pltpu.VMEM)
SMEM = pl.BlockSpec(memory_space=pltpu.SMEM)
NT_DIMS = (((1,), (1,)), ((), ()))
NN_DIMS = (((1,), (0,)), ((), ()))
TN_DIMS = (((0,), (0,)), ((), ()))


def dot(a, b, dims=NN_DIMS):
    return lax.dot_general(a, b, dims, preferred_element_type=f32)


def split(x):
    hi = x.astype(bf16)
    return hi, (x - hi.astype(f32)).astype(bf16)


def call(kernel, outs, flops, moved, specs, scratch=(), grant=12):
    return pl.pallas_call(
        kernel,
        out_shape=outs,
        in_specs=specs,
        out_specs=jax.tree.map(lambda _: VMEM, outs),
        scratch_shapes=scratch,
        compiler_params=pltpu.CompilerParams(vmem_limit_bytes=grant * 2**20),
        cost_estimate=pl.CostEstimate(flops=flops, bytes_accessed=moved, transcendentals=0),
    )


def regroup(piece):
    return [jnp.concatenate([piece(g, k) for g in range(G)], 1) for k in range(4)]


def prepare_kernel(scale_ref, w_ref, tiles_ref, w_out, hi_out, lo_out, held, sems):
    copies = [pltpu.make_async_copy(tiles_ref.at[t], held.at[t], sems.at[t]) for t in range(TR)]
    for copy in copies:
        copy.start()
    rows = [w_ref[c * W + g * 8:c * W + g * 8 + 8, :] for g in range(G) for c in range(C)]
    hi, lo = split(jnp.concatenate(rows, 0))
    old = lax.broadcasted_iota(jnp.int32, (F, F), 0)
    new = lax.broadcasted_iota(jnp.int32, (F, F), 1)
    source = ((new // 8) % C) * W + (new // (8 * C)) * 8 + new % 8
    order = jnp.where(old == source, 1.0, 0.0).astype(bf16)
    w_out[0] = dot(hi, order).astype(bf16)
    w_out[1] = dot(lo, order).astype(bf16)
    for t in range(TR):
        copies[t].wait()
        for s in range(K):
            hi, lo = split(held[t, s] * scale_ref[t, s])
            hi_out[t, :, T * s:T * s + T] = hi
            lo_out[t, :, T * s:T * s + T] = lo


def place(pos_ref, col, sending):
    yh, z = pos_ref[0], pos_ref[1]
    rel_q = ((col // 4) % 4 - z % 4 + 4) % 4
    rel_y = (col // 64 - yh + 2) % 2
    rel_m = ((col // 16) % 4 - ring_peer(z, rel_q, rel_y, sending) // 4 + 4) % 4
    return rel_q * 8 + rel_y * 4 + rel_m


def ring_peer(z, rel_q, rel_y, sending):
    two = 2 - 4 * rel_y if sending else 4 * rel_y - 2
    by = jnp.where(rel_q == 3, -1, jnp.where(rel_q == 2, two, rel_q))
    return (z + by + 16) % 16


def gather_kernel(cols_ref, pos_ref, y0, y1, p0, p1, m0, m1, t0, t1, hi_ref, lo_ref, cot_ref, out_ref, held):
    for at, ref in enumerate((y0, y1, p0, p1, t0, t1, m0, m1)):
        for m in range(4):
            for g in range(G):
                held[at * 4 + m, :, 8 * g:8 * g + 8, :] = ref[m, g]
    for t in range(TR):
        picked = []
        for s in range(K):
            col = cols_ref[t, s]
            picked.append(held[place(pos_ref, col, False), col % 4])
        left_hi, left_lo = split(jnp.concatenate(picked, 1))
        both = dot(jnp.concatenate([left_hi, left_lo], 0), hi_ref[t], NT_DIMS)
        agg = both[:W] + both[W:] + dot(left_hi, lo_ref[t], NT_DIMS)
        parts = regroup(lambda g, k: agg[8 * g:8 * g + 8, W * k:W * k + W])
        cots = regroup(lambda g, k: cot_ref[8 * g:8 * g + 8, T * t + W * k:T * t + W * k + W])
        for k in range(4):
            out_ref[4 * t + k, 0:8, :] = parts[k]
            out_ref[4 * t + k, 8:16, :] = cots[k]


def node_rows(block):
    turned = block.reshape(T, T).T
    return jnp.concatenate([turned[W * g:W * g + W] for g in range(G)], 1)


def node_cols(rows):
    turned = jnp.concatenate([rows[:, T * g:T * g + T] for g in range(G)], 0)
    return turned.T.reshape(C, 8, T)


def layer_kernel(in_ref, w_ref, out_ref):
    agg = node_rows(in_ref[:, 0:8, :])
    cot = node_rows(in_ref[:, 8:16, :])
    agg_hi, agg_lo = split(agg)
    both = dot(jnp.concatenate([agg_hi, agg_lo], 0), w_ref[0])
    pre = both[:W] + both[W:] + dot(agg_hi, w_ref[1])
    sig = jax.nn.sigmoid(pre)
    act = pre * sig
    grad = cot * (sig + act * (1.0 - sig))
    grad_hi, grad_lo = split(grad)
    both = dot(jnp.concatenate([grad_hi, grad_lo], 0), w_ref[0], NT_DIMS)
    back = both[:W] + both[W:] + dot(grad_hi, w_ref[1], NT_DIMS)
    out_ref[:, 0:8, :] = node_cols(back)
    out_ref[:, 8:16, :] = node_cols(act)
    left = jnp.concatenate([agg_hi, agg_lo, agg_hi], 0)
    right = jnp.concatenate([grad_hi, grad_hi, grad_lo], 0)
    for g in range(G):
        part = dot(left[:, T * g:T * g + T], right, TN_DIMS)
        for h in range(4):
            at = 16 + (4 * g + h) * 8
            out_ref[:, at:at + 8, :] = part[:, T * h:T * h + T].reshape(C, 8, T)


def spread_kernel(cols_ref, pos_ref, in_ref, hi_ref, lo_ref, act_ref, out_ref, weight_part):
    yh, z = pos_ref[0], pos_ref[1]
    total = in_ref[0, 16:16 + T, :]
    for c in range(1, C):
        total = total + in_ref[c, 16:16 + T, :]
    weight_part[...] = total.T
    out_ref[:, 0:TR * W, :] = jnp.zeros((32, TR * W, T), f32)
    for q in range(4):
        for y in range(2):
            for m in range(4):
                far = (m + ring_peer(z, q, y, True) // 4) % 4
                block = ((yh + y) % 2) * 16 + far * 4 + (z + q) % 4
                start = pl.multiple_of((block // 2) * 8, 8)
                out_ref[q * 8 + y * 4 + m, TR * W:BLK, :] = weight_part[pl.ds(start, 8), :]
    for t in range(TR):
        grad = regroup(lambda k, g: in_ref[4 * t + k, 0:8, W * g:W * g + W])
        act = regroup(lambda k, g: in_ref[4 * t + k, 8:16, W * g:W * g + W])
        act_ref[:, T * t:T * t + T] = jnp.concatenate(act, 0)
        grad_hi, grad_lo = split(jnp.concatenate(grad, 0))
        both = dot(jnp.concatenate([grad_hi, grad_lo], 0), hi_ref[t])
        sent = both[:W] + both[W:] + dot(grad_hi, lo_ref[t])
        for s in range(K):
            col = cols_ref[t, s]
            block = place(pos_ref, col, True)
            at = pl.ds(pl.multiple_of((col % 4) * W, W), W)
            out_ref[block, at, :] = out_ref[block, at, :] + sent[:, T * s:T * s + T]


def last_kernel(pos_ref, own_ref, up_ref, down_ref, grad_ref, weight_ref):
    total = own_ref[...] + up_ref[...] + down_ref[...]
    for t in range(TR):
        grad_ref[:, T * t:T * t + T] = total[W * t:W * t + W]
    piece = total[TR * W:BLK]
    odd = jnp.concatenate([piece[:, 16:], piece[:, :16]], 1)
    piece = jnp.where(pos_ref[1] % 2 == 1, odd, piece)
    for h in range(2):
        cut = [piece[:, W * g + 8 * h:W * g + 8 * h + 8] for g in range(G)]
        weight_ref[8 * h:8 * h + 8, :] = jnp.concatenate(cut, 1)


def shift(size, by):
    return [(i, (i + by) % size) for i in range(size)]


def along(x, by):
    return lax.ppermute(x, RING, shift(16, by))


def across(x):
    return lax.ppermute(x, "yh", shift(2, 1))


def local(features, weight, tile_cols, tile_count, tile_values, cotangent):
    counts = tile_count.astype(f32)
    slots = lax.broadcasted_iota(jnp.int32, (TR, K), 1)
    scales = jnp.where(slots < tile_count[:, None], 1.0, 0.0) / jnp.sqrt(counts)[:, None]
    pos = jnp.stack([lax.axis_index("yh"), lax.axis_index(RING)]).astype(jnp.int32)
    shape = jax.ShapeDtypeStruct

    with jax.named_scope("gather_features"):
        mine = features.T.reshape(G, 8, TR, T).transpose(0, 2, 1, 3)
        down = along(mine, 4)
        up = along(mine, -4)
        half_up = along(down[:2], 4)
        half_down = along(up[2:], -4)
        y0 = jnp.stack([mine, up, jnp.concatenate([half_up, half_down]), down])
        y1 = across(y0)
        t0, m0, p0 = along(y0, 2), along(y0, 1), along(y0, -1)
        t1, m1, p1 = along(y1, -2), along(y1, 1), along(y1, -1)
    weight_parts, tiles_hi, tiles_lo = call(
        prepare_kernel,
        (shape((2, F, F), bf16), shape((TR, T, K * T), bf16), shape((TR, T, K * T), bf16)),
        4 * F**3, 8 * 2**20, [SMEM, VMEM, pl.BlockSpec(memory_space=pl.ANY)],
        [pltpu.VMEM((TR, K, T, T), f32), pltpu.SemaphoreType.DMA((TR,))], 20,
    )(scales, weight, tile_values)
    packed = call(
        gather_kernel, shape((C, 16, T), f32), 10**8, 6 * 2**20, [SMEM] * 2 + [VMEM] * 11,
        [pltpu.VMEM((32, TR, W, T), f32)],
    )(tile_cols, pos, y0, y1, p0, p1, m0, m1, t0, t1, tiles_hi, tiles_lo, cotangent.T)
    with jax.named_scope("to_nodes"):
        packed = lax.all_to_all(packed, COLS, 0, 0)
    layer = call(layer_kernel, shape((C, 16 + T, T), f32), 10**8, 3 * 2**20, [VMEM] * 2)(packed, weight_parts)
    with jax.named_scope("to_features"):
        layer = lax.all_to_all(layer, COLS, 0, 0)
    activated, parts = call(
        spread_kernel, (shape((W, TR * T), f32), shape((32, BLK, T), f32)), 10**8, 7 * 2**20,
        [SMEM] * 2 + [VMEM] * 3, [pltpu.VMEM((T, T), f32)],
    )(tile_cols, pos, layer, tiles_hi, tiles_lo)
    with jax.named_scope("add_blocks"):
        parts = parts.reshape(4, 2, 4, BLK, T)
        t1, m1, p1 = along(parts[2, 1], -2), along(parts[1, 1], 1), along(parts[3, 1], -1)
        t0, m0, p0 = along(parts[2, 0], 2), along(parts[1, 0], 1), along(parts[3, 0], -1)
        y1 = across(parts[0, 1] + t1 + m1 + p1)
        y0 = parts[0, 0] + t0 + m0 + p0 + y1
        half_up = along(y0[2, :64], 4)
        half_down = along(y0[2, 64:], -4)
        up = along(jnp.concatenate([y0[1, :64] + half_up, y0[1, 64:]]), 4)
        down = along(jnp.concatenate([y0[3, :64], y0[3, 64:] + half_down]), -4)
    grad_features, grad_weight = call(
        last_kernel, (shape((W, TR * T), f32), shape((16, W), f32)), 10**6, 2**19, [SMEM] + [VMEM] * 3,
    )(pos, y0[0], up, down)
    return activated.T, grad_features.T, grad_weight.T


def solution(mesh):
    grid = Mesh(mesh.devices.reshape(2, 4, 4, 2, 4, 2), ROWS + COLS)
    return jax.shard_map(
        local,
        mesh=grid,
        in_specs=(P(ROWS, COLS), P(), P(ROWS, None), P(ROWS), P(ROWS, None, None, None), P(ROWS, COLS)),
        out_specs=(P(ROWS, COLS), P(ROWS, COLS), P(COLS, ROWS)),
        check_vma=False,
    )
```

```python
import jax
import jax.numpy as jnp
from jax import lax
from jax.experimental import pallas as pl
from jax.experimental.pallas import tpu as pltpu
from jax.sharding import Mesh, PartitionSpec as P

ROWS = ("yh", "zh", "zl")
RING = ("zh", "zl")
COLS = ("yl", "x", "core")
PLANE = ("yh",) + COLS
F = 512
W = 32
T = 128
K = 12
TR = 4
C = 16
G = 4
BLK = TR * W + 8
f32, bf16 = jnp.float32, jnp.bfloat16
VMEM = pl.BlockSpec(memory_space=pltpu.VMEM)
SMEM = pl.BlockSpec(memory_space=pltpu.SMEM)
NT_DIMS = (((1,), (1,)), ((), ()))
NN_DIMS = (((1,), (0,)), ((), ()))
TN_DIMS = (((0,), (0,)), ((), ()))


def dot(a, b, dims=NN_DIMS):
    return lax.dot_general(a, b, dims, preferred_element_type=f32)


def split(x):
    hi = x.astype(bf16)
    return hi, (x - hi.astype(f32)).astype(bf16)


def call(kernel, outs, flops, moved, specs, scratch=(), grant=12):
    return pl.pallas_call(
        kernel,
        out_shape=outs,
        in_specs=specs,
        out_specs=jax.tree.map(lambda _: VMEM, outs),
        scratch_shapes=scratch,
        compiler_params=pltpu.CompilerParams(vmem_limit_bytes=grant * 2**20),
        cost_estimate=pl.CostEstimate(flops=flops, bytes_accessed=moved, transcendentals=0),
    )


def regroup(piece):
    return [jnp.concatenate([piece(g, k) for g in range(G)], 1) for k in range(4)]


def prepare_kernel(scale_ref, w_ref, tiles_ref, w_out, hi_out, lo_out, held, sems):
    copies = [pltpu.make_async_copy(tiles_ref.at[t], held.at[t], sems.at[t]) for t in range(TR)]
    for copy in copies:
        copy.start()
    rows = [w_ref[c * W + g * 8:c * W + g * 8 + 8, :] for g in range(G) for c in range(C)]
    hi, lo = split(jnp.concatenate(rows, 0))
    old = lax.broadcasted_iota(jnp.int32, (F, F), 0)
    new = lax.broadcasted_iota(jnp.int32, (F, F), 1)
    source = ((new // 8) % C) * W + (new // (8 * C)) * 8 + new % 8
    order = jnp.where(old == source, 1.0, 0.0).astype(bf16)
    w_out[0] = dot(hi, order).astype(bf16)
    w_out[1] = dot(lo, order).astype(bf16)
    for t in range(TR):
        copies[t].wait()
        for s in range(K):
            hi, lo = split(held[t, s] * scale_ref[t, s])
            hi_out[t, :, T * s:T * s + T] = hi
            lo_out[t, :, T * s:T * s + T] = lo


def source_place(z, col):
    rel_q = ((col // 4) % 4 - z % 4 + 4) % 4
    by = jnp.where(rel_q == 3, -1, jnp.where(rel_q == 2, -2, rel_q))
    return rel_q * 4 + ((col // 16) % 4 - (z + by + 16) % 16 // 4 + 4) % 4


def peer_zh(z, rel_q):
    by = jnp.where(rel_q == 3, -1, rel_q)
    return (z + by + 16) % 16 // 4


def target_place(yh, z, col):
    rel_q = ((col // 4) % 4 - z % 4 + 4) % 4
    rel_m = ((col // 16) % 4 - peer_zh(z, rel_q) + 4) % 4
    return jnp.where(col // 64 == yh, rel_q * 4 + rel_m, 16)


def gather_kernel(
    cols_ref, cols2_ref, scale2_ref, pos_ref, y_ref, p_ref, ta_ref, tb_ref, m_ref, hi_ref, lo_ref, got_ref, other_ref,
    cot_ref, out_ref, hi2_out, lo2_out, held,
):
    yh, z, core = pos_ref[0], pos_ref[1], pos_ref[2]
    for at, ref in ((0, y_ref), (4, p_ref), (8, ta_ref), (10, tb_ref), (12, m_ref)):
        for m in range(ref.shape[0]):
            for g in range(G):
                held[at + m, :, 8 * g:8 * g + 8, :] = ref[m, g]

    def aggregate(cols, t, hi, lo):
        picked = []
        for s in range(K):
            col = cols[t, s]
            mine = jnp.where(col // 64 == yh, 1.0, 0.0).astype(f32)
            picked.append(held[source_place(z, col), col % 4] * mine)
        left_hi, left_lo = split(jnp.concatenate(picked, 1))
        both = dot(jnp.concatenate([left_hi, left_lo], 0), hi, NT_DIMS)
        agg = both[:W] + both[W:] + dot(left_hi, lo, NT_DIMS)
        return regroup(lambda g, k: agg[8 * g:8 * g + 8, W * k:W * k + W])

    for t in range(TR):
        parts = aggregate(cols_ref, t, hi_ref[t], lo_ref[t])
        cots = regroup(lambda g, k: cot_ref[8 * g:8 * g + 8, T * t + W * k:T * t + W * k + W])
        for k in range(4):
            out_ref[yh * C + 4 * t + k, 0:8, :] = parts[k]
            out_ref[yh * C + 4 * t + k, 8:16, :] = cots[k]
    for j in range(TR):
        t = (2 * core + j) % 4
        ref = got_ref if j < 2 else other_ref
        pairs = [split(ref[j % 2, s] * scale2_ref[t, s]) for s in range(K)]
        hi2_out[j] = jnp.concatenate([p[0] for p in pairs], 1)
        lo2_out[j] = jnp.concatenate([p[1] for p in pairs], 1)
        parts = aggregate(cols2_ref, t, hi2_out[j], lo2_out[j])
        for k in range(4):
            out_ref[(1 - yh) * C + 4 * t + k, 0:8, :] = parts[k]
            out_ref[(1 - yh) * C + 4 * t + k, 8:16, :] = jnp.zeros((8, T), f32)


def node_rows(block):
    turned = block.reshape(T, T).T
    return jnp.concatenate([turned[W * g:W * g + W] for g in range(G)], 1)


def node_cols(rows):
    turned = jnp.concatenate([rows[:, T * g:T * g + T] for g in range(G)], 0)
    return turned.T.reshape(C, 8, T)


def layer_kernel(pos_ref, in_ref, w_ref, out_ref):
    agg = node_rows(in_ref[0:C, 0:8, :] + in_ref[C:2 * C, 0:8, :])
    cot = node_rows(in_ref[pl.ds(pos_ref[0] * C, C), 8:16, :])
    agg_hi, agg_lo = split(agg)
    both = dot(jnp.concatenate([agg_hi, agg_lo], 0), w_ref[0])
    pre = both[:W] + both[W:] + dot(agg_hi, w_ref[1])
    sig = jax.nn.sigmoid(pre)
    act = pre * sig
    grad = cot * (sig + act * (1.0 - sig))
    grad_hi, grad_lo = split(grad)
    both = dot(jnp.concatenate([grad_hi, grad_lo], 0), w_ref[0], NT_DIMS)
    back = both[:W] + both[W:] + dot(grad_hi, w_ref[1], NT_DIMS)
    for out, at in ((node_cols(back), 0), (node_cols(act), 8)):
        out_ref[0:C, at:at + 8, :] = out
        out_ref[C:2 * C, at:at + 8, :] = out
    left = jnp.concatenate([agg_hi, agg_lo, agg_hi], 0)
    right = jnp.concatenate([grad_hi, grad_hi, grad_lo], 0)
    for g in range(G):
        part = dot(left[:, T * g:T * g + T], right, TN_DIMS)
        for y in range(2):
            for h in range(2):
                cuts = [part[:, T * (2 * h + j) + 64 * y:T * (2 * h + j) + 64 * y + 64] for j in range(2)]
                at = 16 + (2 * g + h) * 8
                out_ref[C * y:C * y + C, at:at + 8, :] = jnp.concatenate(cuts, 1).reshape(C, 8, T)


def spread_kernel(cols_ref, cols2_ref, pos_ref, in_ref, hi_ref, lo_ref, hi2_ref, lo2_ref, act_ref, out_ref, weight_part):
    yh, z, core = pos_ref[0], pos_ref[1], pos_ref[2]
    total = in_ref[0, 16:80, :]
    for c in range(1, 2 * C):
        total = total + in_ref[c, 16:80, :]
    turned = total.T
    weight_part[...] = jnp.concatenate([turned[:64], turned[64:]], 1)
    out_ref[:, 0:TR * W, :] = jnp.zeros((17, TR * W, T), f32)
    for q in range(4):
        for m in range(4):
            target = (m + peer_zh(z, q)) % 4 * 4 + (z + q) % 4
            start = pl.multiple_of((target // 2) * 8, 8)
            out_ref[q * 4 + m, TR * W:BLK, :] = weight_part[pl.ds(start, 8), :]

    def spread(cols, t, y, hi, lo):
        grad = regroup(lambda k, g: in_ref[y * C + 4 * t + k, 0:8, :][:, W * g:W * g + W])
        grad_hi, grad_lo = split(jnp.concatenate(grad, 0))
        both = dot(jnp.concatenate([grad_hi, grad_lo], 0), hi)
        sent = both[:W] + both[W:] + dot(grad_hi, lo)
        for s in range(K):
            col = cols[t, s]
            block = target_place(yh, z, col)
            at = pl.ds(pl.multiple_of((col % 4) * W, W), W)
            out_ref[block, at, :] = out_ref[block, at, :] + sent[:, T * s:T * s + T]

    for t in range(TR):
        act = regroup(lambda k, g: in_ref[yh * C + 4 * t + k, 8:16, :][:, W * g:W * g + W])
        act_ref[:, T * t:T * t + T] = jnp.concatenate(act, 0)
        spread(cols_ref, t, yh, hi_ref[t], lo_ref[t])
    for j in range(TR):
        spread(cols2_ref, (2 * core + j) % 4, 1 - yh, hi2_ref[j], lo2_ref[j])


def last_kernel(pos_ref, own_ref, up_ref, down_ref, grad_ref, weight_ref):
    total = own_ref[...] + up_ref[...] + down_ref[...]
    for t in range(TR):
        grad_ref[:, T * t:T * t + T] = total[W * t:W * t + W]
    piece = total[TR * W:BLK]
    odd = jnp.concatenate([piece[:, 8:], piece[:, :8]], 1)
    piece = jnp.where(pos_ref[1] % 2 == 1, odd, piece)
    for h in range(2):
        cut = [piece[:, 64 * h + 16 * g:64 * h + 16 * g + 8] for g in range(G)]
        weight_ref[8 * h:8 * h + 8, :] = jnp.concatenate(cut, 1)


def shift(size, by):
    return [(i, (i + by) % size) for i in range(size)]


def along(x, by):
    return lax.ppermute(x, RING, shift(16, by))


def across(x):
    return lax.ppermute(x, "yh", shift(2, 1))


def local(features, weight, tile_cols, tile_count, tile_values, cotangent):
    counts = tile_count.astype(f32)
    slots = lax.broadcasted_iota(jnp.int32, (TR, K), 1)
    scales = jnp.where(slots < tile_count[:, None], 1.0, 0.0) / jnp.sqrt(counts)[:, None]
    places = [lax.axis_index("yh"), lax.axis_index(RING), lax.axis_index("core")]
    pos = jnp.stack(places).astype(jnp.int32)
    shape = jax.ShapeDtypeStruct

    with jax.named_scope("swap_tiles"):
        half = lax.dynamic_slice_in_dim(tile_values, 2 * places[2], 2, 0)
        got = across(half)
        facts = across(jnp.stack([tile_cols.astype(f32), scales]))
        cols2, scales2 = facts[0].astype(jnp.int32), facts[1]
    with jax.named_scope("gather_features"):
        mine = features.T.reshape(G, 8, TR, T).transpose(0, 2, 1, 3)
        down = along(mine, 4)
        up = along(mine, -4)
        half_up = along(down[:2], 4)
        half_down = along(up[2:], -4)
        far = jnp.stack([mine, up, jnp.concatenate([half_up, half_down]), down])
        ta, tb = along(far[:2], 2), along(far[1:3], -2)
        m, p = along(far, 1), along(far, -1)
    with jax.named_scope("swap_cores"):
        got, ta, tb, m, p = lax.optimization_barrier((got, ta, tb, m, p))
        other = lax.ppermute(got, "core", shift(2, 1))
    weight_parts, tiles_hi, tiles_lo = call(
        prepare_kernel,
        (shape((2, F, F), bf16), shape((TR, T, K * T), bf16), shape((TR, T, K * T), bf16)),
        4 * F**3, 8 * 2**20, [SMEM, VMEM, pl.BlockSpec(memory_space=pl.ANY)],
        [pltpu.VMEM((TR, K, T, T), f32), pltpu.SemaphoreType.DMA((TR,))], 20,
    )(scales, weight, tile_values)
    packed, tiles2_hi, tiles2_lo = call(
        gather_kernel,
        (shape((2 * C, 16, T), f32), shape((TR, T, K * T), bf16), shape((TR, T, K * T), bf16)),
        10**8, 9 * 2**20, [SMEM] * 4 + [VMEM] * 10, [pltpu.VMEM((16, TR, W, T), f32)], 16,
    )(tile_cols, cols2, scales2, pos, far, p, ta, tb, m, tiles_hi, tiles_lo, got, other, cotangent.T)
    with jax.named_scope("to_nodes"):
        packed = lax.all_to_all(packed, PLANE, 0, 0)
    layer = call(layer_kernel, shape((2 * C, 80, T), f32), 10**8, 3 * 2**20, [SMEM] + [VMEM] * 2)(
        pos, packed, weight_parts
    )
    with jax.named_scope("to_features"):
        layer = lax.all_to_all(layer, PLANE, 0, 0)
    activated, parts = call(
        spread_kernel, (shape((W, TR * T), f32), shape((17, BLK, T), f32)), 10**8, 7 * 2**20,
        [SMEM] * 3 + [VMEM] * 5, [pltpu.VMEM((64, T), f32)], 16,
    )(tile_cols, cols2, pos, layer, tiles_hi, tiles_lo, tiles2_hi, tiles2_lo)
    with jax.named_scope("add_blocks"):
        ta, tb = along(parts[8:10], 2), along(parts[10:12], -2)
        m, p = along(parts[4:8], 1), along(parts[12:16], -1)
        own = parts[:4] + m + p
        two = own[2]
        half_up = along(two[:64], 4)
        half_down = along(two[64:], -4)
        one, three = own[1] + ta[1], own[3] + tb[0]
        up = along(jnp.concatenate([one[:64] + half_up, one[64:]]), 4)
        down = along(jnp.concatenate([three[:64], three[64:] + half_down]), -4)
        own = own[0] + ta[0] + tb[1]
    grad_features, grad_weight = call(
        last_kernel, (shape((W, TR * T), f32), shape((16, W), f32)), 10**6, 2**19, [SMEM] + [VMEM] * 3,
    )(pos, own, up, down)
    return activated.T, grad_features.T, grad_weight.T


def solution(mesh):
    grid = Mesh(mesh.devices.reshape(2, 4, 4, 2, 4, 2), ROWS + COLS)
    return jax.shard_map(
        local,
        mesh=grid,
        in_specs=(P(ROWS, COLS), P(), P(ROWS, None), P(ROWS), P(ROWS, None, None, None), P(ROWS, COLS)),
        out_specs=(P(ROWS, COLS), P(ROWS, COLS), P(COLS, ROWS)),
        check_vma=False,
    )
```

```python
import jax
import jax.numpy as jnp
from jax import lax
from jax.experimental import pallas as pl
from jax.experimental.pallas import tpu as pltpu
from jax.sharding import Mesh, PartitionSpec as P

ROWS = ("yh", "zh", "zl")
RING = ("zh", "zl")
COLS = ("yl", "x", "core")
PLANE = ("yh",) + COLS
F = 512
W = 32
T = 128
K = 12
TR = 4
C = 16
G = 4
BLK = TR * W + 8
f32, bf16 = jnp.float32, jnp.bfloat16
VMEM = pl.BlockSpec(memory_space=pltpu.VMEM)
SMEM = pl.BlockSpec(memory_space=pltpu.SMEM)
NT_DIMS = (((1,), (1,)), ((), ()))
NN_DIMS = (((1,), (0,)), ((), ()))
TN_DIMS = (((0,), (0,)), ((), ()))


def dot(a, b, dims=NN_DIMS):
    return lax.dot_general(a, b, dims, preferred_element_type=f32)


def split(x):
    hi = x.astype(bf16)
    return hi, (x - hi.astype(f32)).astype(bf16)


def call(kernel, outs, flops, moved, specs, scratch=(), grant=12, aliases={}):
    return pl.pallas_call(
        kernel,
        out_shape=outs,
        in_specs=specs,
        out_specs=jax.tree.map(lambda _: VMEM, outs),
        scratch_shapes=scratch,
        input_output_aliases=aliases,
        compiler_params=pltpu.CompilerParams(vmem_limit_bytes=grant * 2**20),
        cost_estimate=pl.CostEstimate(flops=flops, bytes_accessed=moved, transcendentals=0),
    )


def regroup(piece):
    return [jnp.concatenate([piece(g, k) for g in range(G)], 1) for k in range(4)]


def prepare_kernel(scale_ref, w_ref, tiles_ref, w_out, hi_out, lo_out, held, sems):
    copies = [pltpu.make_async_copy(tiles_ref.at[t], held.at[t], sems.at[t]) for t in range(TR)]
    for copy in copies:
        copy.start()
    rows = [w_ref[c * W + g * 8:c * W + g * 8 + 8, :] for g in range(G) for c in range(C)]
    hi, lo = split(jnp.concatenate(rows, 0))
    old = lax.broadcasted_iota(jnp.int32, (F, F), 0)
    new = lax.broadcasted_iota(jnp.int32, (F, F), 1)
    source = ((new // 8) % C) * W + (new // (8 * C)) * 8 + new % 8
    order = jnp.where(old == source, 1.0, 0.0).astype(bf16)
    w_out[0] = dot(hi, order).astype(bf16)
    w_out[1] = dot(lo, order).astype(bf16)
    for t in range(TR):
        copies[t].wait()
        for s in range(K):
            hi, lo = split(held[t, s] * scale_ref[t, s])
            hi_out[t, :, T * s:T * s + T] = hi
            lo_out[t, :, T * s:T * s + T] = lo


def source_place(z, col):
    return ((col // 4) % 4 - z % 4 + 4) % 4 * 4 + (col // 16) % 4


def peer_zh(z, rel_q):
    by = jnp.where(rel_q == 3, -1, rel_q)
    return (z + by + 16) % 16 // 4


def target_place(yh, z, col):
    rel_q = ((col // 4) % 4 - z % 4 + 4) % 4
    rel_m = ((col // 16) % 4 - peer_zh(z, rel_q) + 4) % 4
    return jnp.where(col // 64 == yh, rel_q * 4 + rel_m, 16)


def aggregate(held, pos_ref, cols, t, hi, lo):
    picked = []
    for s in range(K):
        col = cols[t, s]
        mine = jnp.where(col // 64 == pos_ref[0], 1.0, 0.0).astype(f32)
        picked.append(held[source_place(pos_ref[1], col), col % 4] * mine)
    left_hi, left_lo = split(jnp.concatenate(picked, 1))
    both = dot(jnp.concatenate([left_hi, left_lo], 0), hi, NT_DIMS)
    agg = both[:W] + both[W:] + dot(left_hi, lo, NT_DIMS)
    return regroup(lambda g, k: agg[8 * g:8 * g + 8, W * k:W * k + W])


def aggregate_other(first, tiles_ref, held, pos_ref, cols_ref, scale_ref, out_ref, hi_out, lo_out):
    for j in range(2):
        t = (2 * pos_ref[2] + j + (0 if first else 2)) % 4
        pairs = [split(tiles_ref[K * j + s] * scale_ref[t, s]) for s in range(K)]
        hi_out[j] = jnp.concatenate([p[0] for p in pairs], 1)
        lo_out[j] = jnp.concatenate([p[1] for p in pairs], 1)
        parts = aggregate(held, pos_ref, cols_ref, t, hi_out[j], lo_out[j])
        for k in range(4):
            at = (1 - pos_ref[0]) * C + 4 * t + k
            out_ref[at, 0:8, :] = parts[k]
            out_ref[at, 8:16, :] = jnp.zeros((8, T), f32)


def gather_kernel(
    cols_ref, cols2_ref, scale2_ref, pos_ref, y_ref, p_ref, ta_ref, tb_ref, m_ref, hi_ref, lo_ref, got_ref,
    cot_ref, out_ref, hi2_out, lo2_out, held,
):
    for at, ref in ((0, y_ref), (4, p_ref), (8, ta_ref), (10, tb_ref), (12, m_ref)):
        for m in range(ref.shape[0]):
            held[at + m] = ref[m]
    for t in range(TR):
        parts = aggregate(held, pos_ref, cols_ref, t, hi_ref[t], lo_ref[t])
        cots = regroup(lambda g, k: cot_ref[8 * g:8 * g + 8, T * t + W * k:T * t + W * k + W])
        for k in range(4):
            out_ref[pos_ref[0] * C + 4 * t + k, 0:8, :] = parts[k]
            out_ref[pos_ref[0] * C + 4 * t + k, 8:16, :] = cots[k]
    aggregate_other(True, got_ref, held, pos_ref, cols2_ref, scale2_ref, out_ref, hi2_out, lo2_out)


def gather_rest_kernel(cols2_ref, scale2_ref, pos_ref, held, other_ref, in_ref, out_ref, hi2_out, lo2_out):
    aggregate_other(False, other_ref, held, pos_ref, cols2_ref, scale2_ref, out_ref, hi2_out, lo2_out)


def node_rows(block):
    turned = block.reshape(T, T).T
    return jnp.concatenate([turned[W * g:W * g + W] for g in range(G)], 1)


def node_cols(rows):
    turned = jnp.concatenate([rows[:, T * g:T * g + T] for g in range(G)], 0)
    return turned.T.reshape(C, 8, T)


def layer_kernel(pos_ref, in_ref, w_ref, out_ref):
    agg = node_rows(in_ref[0:C, 0:8, :] + in_ref[C:2 * C, 0:8, :])
    cot = node_rows(in_ref[pl.ds(pos_ref[0] * C, C), 8:16, :])
    agg_hi, agg_lo = split(agg)
    both = dot(jnp.concatenate([agg_hi, agg_lo], 0), w_ref[0])
    pre = both[:W] + both[W:] + dot(agg_hi, w_ref[1])
    sig = jax.nn.sigmoid(pre)
    act = pre * sig
    grad = cot * (sig + act * (1.0 - sig))
    grad_hi, grad_lo = split(grad)
    both = dot(jnp.concatenate([grad_hi, grad_lo], 0), w_ref[0], NT_DIMS)
    back = both[:W] + both[W:] + dot(grad_hi, w_ref[1], NT_DIMS)
    for out, at in ((node_cols(back), 0), (node_cols(act), 8)):
        out_ref[0:C, at:at + 8, :] = out
        out_ref[C:2 * C, at:at + 8, :] = out
    left = jnp.concatenate([agg_hi, agg_lo, agg_hi], 0)
    right = jnp.concatenate([grad_hi, grad_hi, grad_lo], 0)
    for g in range(G):
        part = dot(left[:, T * g:T * g + T], right, TN_DIMS)
        for y in range(2):
            for h in range(2):
                cuts = [part[:, T * (2 * h + j) + 64 * y:T * (2 * h + j) + 64 * y + 64] for j in range(2)]
                at = 16 + (2 * g + h) * 8
                out_ref[C * y:C * y + C, at:at + 8, :] = jnp.concatenate(cuts, 1).reshape(C, 8, T)


def spread_kernel(
    cols_ref, cols2_ref, pos_ref, in_ref, hi_ref, lo_ref, hi2_ref, lo2_ref, hi3_ref, lo3_ref, act_ref, out_ref, weight_part,
):
    yh, z, core = pos_ref[0], pos_ref[1], pos_ref[2]
    total = in_ref[0, 16:80, :]
    for c in range(1, 2 * C):
        total = total + in_ref[c, 16:80, :]
    turned = total.T
    weight_part[...] = jnp.concatenate([turned[:64], turned[64:]], 1)
    out_ref[:, 0:TR * W, :] = jnp.zeros((17, TR * W, T), f32)
    for q in range(4):
        for m in range(4):
            target = (m + peer_zh(z, q)) % 4 * 4 + (z + q) % 4
            start = pl.multiple_of((target // 2) * 8, 8)
            out_ref[q * 4 + m, TR * W:BLK, :] = weight_part[pl.ds(start, 8), :]

    def spread(cols, t, y, hi, lo):
        grad = regroup(lambda k, g: in_ref[y * C + 4 * t + k, 0:8, :][:, W * g:W * g + W])
        grad_hi, grad_lo = split(jnp.concatenate(grad, 0))
        both = dot(jnp.concatenate([grad_hi, grad_lo], 0), hi)
        sent = both[:W] + both[W:] + dot(grad_hi, lo)
        for s in range(K):
            col = cols[t, s]
            block = target_place(yh, z, col)
            at = pl.ds(pl.multiple_of((col % 4) * W, W), W)
            out_ref[block, at, :] = out_ref[block, at, :] + sent[:, T * s:T * s + T]

    for t in range(TR):
        act = regroup(lambda k, g: in_ref[yh * C + 4 * t + k, 8:16, :][:, W * g:W * g + W])
        act_ref[:, T * t:T * t + T] = jnp.concatenate(act, 0)
        spread(cols_ref, t, yh, hi_ref[t], lo_ref[t])
    for j in range(TR):
        hi, lo = (hi2_ref, lo2_ref) if j < 2 else (hi3_ref, lo3_ref)
        spread(cols2_ref, (2 * core + j) % 4, 1 - yh, hi[j % 2], lo[j % 2])


def last_kernel(pos_ref, own_ref, up_ref, down_ref, grad_ref, weight_ref):
    total = own_ref[...] + up_ref[...] + down_ref[...]
    for t in range(TR):
        grad_ref[:, T * t:T * t + T] = total[W * t:W * t + W]
    piece = total[TR * W:BLK]
    odd = jnp.concatenate([piece[:, 8:], piece[:, :8]], 1)
    piece = jnp.where(pos_ref[1] % 2 == 1, odd, piece)
    for h in range(2):
        cut = [piece[:, 64 * h + 16 * g:64 * h + 16 * g + 8] for g in range(G)]
        weight_ref[8 * h:8 * h + 8, :] = jnp.concatenate(cut, 1)


def shift(size, by):
    return [(i, (i + by) % size) for i in range(size)]


def along(x, by):
    return lax.ppermute(x, RING, shift(16, by))


def across(x):
    return lax.ppermute(x, "yh", shift(2, 1))


def tile_scales(tile_count):
    counts = tile_count.astype(f32)
    slots = lax.broadcasted_iota(jnp.int32, (TR, K), 1)
    return jnp.where(slots < tile_count[:, None], 1.0, 0.0) / jnp.sqrt(counts)[:, None]


def local(features, weight, tile_cols, tile_count, tile_values, cotangent):
    scales = tile_scales(tile_count)
    places = [lax.axis_index("yh"), lax.axis_index(RING), lax.axis_index("core")]
    pos = jnp.stack(places).astype(jnp.int32)
    shape = jax.ShapeDtypeStruct

    with jax.named_scope("swap_tiles"):
        half = lax.dynamic_slice_in_dim(tile_values, 2 * places[2], 2, 0).reshape(2 * K, T, T)
        facts = jnp.concatenate([tile_cols.astype(f32), tile_count.astype(f32)[:, None]], 1)
        facts = jnp.pad(facts, ((0, T - TR), (0, T - K - 1)))
        got = across(jnp.concatenate([half, facts[None]]))
        cols2 = got[2 * K, :TR, :K].astype(jnp.int32)
        scales2 = tile_scales(got[2 * K, :TR, K].astype(jnp.int32))
    with jax.named_scope("gather_features"):
        mine = features.T.reshape(W, TR, T).transpose(1, 0, 2)
        far = lax.all_to_all(jnp.stack([mine] * 4), "zh", 0, 0)
        ta, tb = along(far[:2], 2), along(far[2:], -2)
        m, p = along(far, 1), along(far, -1)
    weight_parts, tiles_hi, tiles_lo = call(
        prepare_kernel,
        (shape((2, F, F), bf16), shape((TR, T, K * T), bf16), shape((TR, T, K * T), bf16)),
        4 * F**3, 8 * 2**20, [SMEM, VMEM, pl.BlockSpec(memory_space=pl.ANY)],
        [pltpu.VMEM((TR, K, T, T), f32), pltpu.SemaphoreType.DMA((TR,))], 12,
    )(scales, weight, tile_values)
    with jax.named_scope("swap_cores"):
        last = ta[0, 0, 0, 0] + tb[0, 0, 0, 0] + m[0, 0, 0, 0] + p[0, 0, 0, 0]
        last = last + weight_parts[0, 0, 0].astype(f32)
        other = lax.ppermute(got[:2 * K] * (last * 0.0 + 1.0), "core", shift(2, 1))
    wide = shape((2, T, K * T), bf16)
    sent = shape((2 * C, 16, T), f32)
    packed, tiles2_hi, tiles2_lo, held = call(
        gather_kernel, (sent, wide, wide, shape((16, TR, W, T), f32)), 10**8, 7 * 2**20, [SMEM] * 4 + [VMEM] * 9,
    )(tile_cols, cols2, scales2, pos, far, p, ta, tb, m, tiles_hi, tiles_lo, got, cotangent.T)
    packed, tiles3_hi, tiles3_lo = call(
        gather_rest_kernel, (sent, wide, wide), 10**8, 5 * 2**20, [SMEM] * 3 + [VMEM] * 3, aliases={5: 0},
    )(cols2, scales2, pos, held, other, packed)
    with jax.named_scope("to_nodes"):
        packed = lax.all_to_all(packed, PLANE, 0, 0)
    layer = call(layer_kernel, shape((2 * C, 80, T), f32), 10**8, 3 * 2**20, [SMEM] + [VMEM] * 2)(
        pos, packed, weight_parts
    )
    with jax.named_scope("to_features"):
        layer = lax.all_to_all(layer, PLANE, 0, 0)
    activated, parts = call(
        spread_kernel, (shape((W, TR * T), f32), shape((17, BLK, T), f32)), 10**8, 7 * 2**20,
        [SMEM] * 3 + [VMEM] * 7, [pltpu.VMEM((64, T), f32)],
    )(tile_cols, cols2, pos, layer, tiles_hi, tiles_lo, tiles2_hi, tiles2_lo, tiles3_hi, tiles3_lo)
    with jax.named_scope("add_blocks"):
        ta, tb = along(parts[8:10], 2), along(parts[10:12], -2)
        m, p = along(parts[4:8], 1), along(parts[12:16], -1)
        own = parts[:4] + m + p
        two = own[2]
        half_up = along(two[:64], 4)
        half_down = along(two[64:], -4)
        one, three = own[1] + ta[1], own[3] + tb[0]
        up = along(jnp.concatenate([one[:64] + half_up, one[64:]]), 4)
        down = along(jnp.concatenate([three[:64], three[64:] + half_down]), -4)
        own = own[0] + ta[0] + tb[1]
    grad_features, grad_weight = call(
        last_kernel, (shape((W, TR * T), f32), shape((16, W), f32)), 10**6, 2**19, [SMEM] + [VMEM] * 3,
    )(pos, own, up, down)
    return activated.T, grad_features.T, grad_weight.T


def solution(mesh):
    grid = Mesh(mesh.devices.reshape(2, 4, 4, 2, 4, 2), ROWS + COLS)
    return jax.shard_map(
        local,
        mesh=grid,
        in_specs=(P(ROWS, COLS), P(), P(ROWS, None), P(ROWS), P(ROWS, None, None, None), P(ROWS, COLS)),
        out_specs=(P(ROWS, COLS), P(ROWS, COLS), P(COLS, ROWS)),
        check_vma=False,
    )
```

```python
import jax
import jax.numpy as jnp
from jax import lax
from jax.experimental import pallas as pl
from jax.experimental.pallas import tpu as pltpu
from jax.sharding import Mesh, PartitionSpec as P

ROWS = ("yh", "zh", "zl")
RING = ("zh", "zl")
COLS = ("yl", "x", "core")
F = 512
W = 32
T = 128
K = 12
TR = 4
C = 16
G = 4
BLK = TR * W + 8
f32, bf16 = jnp.float32, jnp.bfloat16
VMEM = pl.BlockSpec(memory_space=pltpu.VMEM)
SMEM = pl.BlockSpec(memory_space=pltpu.SMEM)
NT_DIMS = (((1,), (1,)), ((), ()))
NN_DIMS = (((1,), (0,)), ((), ()))
TN_DIMS = (((0,), (0,)), ((), ()))


def dot(a, b, dims=NN_DIMS):
    return lax.dot_general(a, b, dims, preferred_element_type=f32)


def split(x):
    hi = x.astype(bf16)
    return hi, (x - hi.astype(f32)).astype(bf16)


def call(kernel, outs, flops, moved, specs, scratch=(), grant=12):
    return pl.pallas_call(
        kernel,
        out_shape=outs,
        in_specs=specs,
        out_specs=jax.tree.map(lambda _: VMEM, outs),
        scratch_shapes=scratch,
        compiler_params=pltpu.CompilerParams(vmem_limit_bytes=grant * 2**20),
        cost_estimate=pl.CostEstimate(flops=flops, bytes_accessed=moved, transcendentals=0),
    )


def regroup(piece):
    return [jnp.concatenate([piece(g, k) for g in range(G)], 1) for k in range(4)]


def prepare_kernel(scale_ref, w_ref, tiles_ref, w_out, hi_out, lo_out, held, sems):
    copies = [pltpu.make_async_copy(tiles_ref.at[t], held.at[t], sems.at[t]) for t in range(TR)]
    for copy in copies:
        copy.start()
    rows = [w_ref[c * W + g * 8:c * W + g * 8 + 8, :] for g in range(G) for c in range(C)]
    hi, lo = split(jnp.concatenate(rows, 0))
    old = lax.broadcasted_iota(jnp.int32, (F, F), 0)
    new = lax.broadcasted_iota(jnp.int32, (F, F), 1)
    source = ((new // 8) % C) * W + (new // (8 * C)) * 8 + new % 8
    order = jnp.where(old == source, 1.0, 0.0).astype(bf16)
    w_out[0] = dot(hi, order).astype(bf16)
    w_out[1] = dot(lo, order).astype(bf16)
    for t in range(TR):
        copies[t].wait()
        for s in range(K):
            hi, lo = split(held[t, s] * scale_ref[t, s])
            hi_out[t, :, T * s:T * s + T] = hi
            lo_out[t, :, T * s:T * s + T] = lo


def near(pos_ref, col):
    return ((col // 4) % 4 - pos_ref[1] % 4 + 4) % 4, (col // 64 - pos_ref[0] + 2) % 2


def source_place(pos_ref, col):
    rel_q, rel_y = near(pos_ref, col)
    return rel_q * 8 + rel_y * 4 + (col // 16) % 4


def target_zh(z, rel_q, rel_y):
    by = jnp.where(rel_q == 3, -1, jnp.where(rel_q == 2, 2 - 4 * rel_y, rel_q))
    return (z + by + 16) % 16 // 4


def target_place(pos_ref, col):
    rel_q, rel_y = near(pos_ref, col)
    return rel_q * 8 + rel_y * 4 + ((col // 16) % 4 - target_zh(pos_ref[1], rel_q, rel_y) + 4) % 4


def gather_kernel(cols_ref, pos_ref, y_ref, p_ref, t0, t1, m_ref, hi_ref, lo_ref, cot_ref, out_ref, held):
    for at, ref in ((0, y_ref), (8, p_ref), (16, t0), (20, t1), (24, m_ref)):
        for m in range(4):
            if len(ref.shape) == 4:
                held[at + m] = ref[m]
            else:
                for y in range(2):
                    held[at + 4 * y + m] = ref[y, m]
    for t in range(TR):
        picked = []
        for s in range(K):
            col = cols_ref[t, s]
            picked.append(held[source_place(pos_ref, col), col % 4])
        left_hi, left_lo = split(jnp.concatenate(picked, 1))
        both = dot(jnp.concatenate([left_hi, left_lo], 0), hi_ref[t], NT_DIMS)
        agg = both[:W] + both[W:] + dot(left_hi, lo_ref[t], NT_DIMS)
        parts = regroup(lambda g, k: agg[8 * g:8 * g + 8, W * k:W * k + W])
        cots = regroup(lambda g, k: cot_ref[8 * g:8 * g + 8, T * t + W * k:T * t + W * k + W])
        for k in range(4):
            out_ref[4 * t + k, 0:8, :] = parts[k]
            out_ref[4 * t + k, 8:16, :] = cots[k]


def node_rows(block):
    turned = block.reshape(T, T).T
    return jnp.concatenate([turned[W * g:W * g + W] for g in range(G)], 1)


def node_cols(rows):
    turned = jnp.concatenate([rows[:, T * g:T * g + T] for g in range(G)], 0)
    return turned.T.reshape(C, 8, T)


def layer_kernel(in_ref, w_ref, out_ref):
    agg = node_rows(in_ref[:, 0:8, :])
    cot = node_rows(in_ref[:, 8:16, :])
    agg_hi, agg_lo = split(agg)
    both = dot(jnp.concatenate([agg_hi, agg_lo], 0), w_ref[0])
    pre = both[:W] + both[W:] + dot(agg_hi, w_ref[1])
    sig = jax.nn.sigmoid(pre)
    act = pre * sig
    grad = cot * (sig + act * (1.0 - sig))
    grad_hi, grad_lo = split(grad)
    both = dot(jnp.concatenate([grad_hi, grad_lo], 0), w_ref[0], NT_DIMS)
    back = both[:W] + both[W:] + dot(grad_hi, w_ref[1], NT_DIMS)
    out_ref[:, 0:8, :] = node_cols(back)
    out_ref[:, 8:16, :] = node_cols(act)
    left = jnp.concatenate([agg_hi, agg_lo, agg_hi], 0)
    right = jnp.concatenate([grad_hi, grad_hi, grad_lo], 0)
    for g in range(G):
        part = dot(left[:, T * g:T * g + T], right, TN_DIMS)
        for h in range(4):
            at = 16 + (4 * g + h) * 8
            out_ref[:, at:at + 8, :] = part[:, T * h:T * h + T].reshape(C, 8, T)


def spread_kernel(cols_ref, pos_ref, in_ref, hi_ref, lo_ref, act_ref, out_ref, weight_part):
    yh, z = pos_ref[0], pos_ref[1]
    total = in_ref[0, 16:16 + T, :]
    for c in range(1, C):
        total = total + in_ref[c, 16:16 + T, :]
    weight_part[...] = total.T
    out_ref[:, 0:TR * W, :] = jnp.zeros((32, TR * W, T), f32)
    for q in range(4):
        for y in range(2):
            for m in range(4):
                far = (m + target_zh(z, q, y)) % 4
                block = ((yh + y) % 2) * 16 + far * 4 + (z + q) % 4
                start = pl.multiple_of((block // 2) * 8, 8)
                out_ref[q * 8 + y * 4 + m, TR * W:BLK, :] = weight_part[pl.ds(start, 8), :]
    for t in range(TR):
        grad = regroup(lambda k, g: in_ref[4 * t + k, 0:8, W * g:W * g + W])
        act = regroup(lambda k, g: in_ref[4 * t + k, 8:16, W * g:W * g + W])
        act_ref[:, T * t:T * t + T] = jnp.concatenate(act, 0)
        grad_hi, grad_lo = split(jnp.concatenate(grad, 0))
        both = dot(jnp.concatenate([grad_hi, grad_lo], 0), hi_ref[t])
        sent = both[:W] + both[W:] + dot(grad_hi, lo_ref[t])
        for s in range(K):
            col = cols_ref[t, s]
            block = target_place(pos_ref, col)
            at = pl.ds(pl.multiple_of((col % 4) * W, W), W)
            out_ref[block, at, :] = out_ref[block, at, :] + sent[:, T * s:T * s + T]


def last_kernel(pos_ref, own_ref, up_ref, down_ref, grad_ref, weight_ref):
    total = own_ref[...] + up_ref[...] + down_ref[...]
    for t in range(TR):
        grad_ref[:, T * t:T * t + T] = total[W * t:W * t + W]
    piece = total[TR * W:BLK]
    odd = jnp.concatenate([piece[:, 16:], piece[:, :16]], 1)
    piece = jnp.where(pos_ref[1] % 2 == 1, odd, piece)
    for h in range(2):
        cut = [piece[:, W * g + 8 * h:W * g + 8 * h + 8] for g in range(G)]
        weight_ref[8 * h:8 * h + 8, :] = jnp.concatenate(cut, 1)


def shift(size, by):
    return [(i, (i + by) % size) for i in range(size)]


def along(x, by):
    return lax.ppermute(x, RING, shift(16, by))


def across(x):
    return lax.ppermute(x, "yh", shift(2, 1))


def local(features, weight, tile_cols, tile_count, tile_values, cotangent):
    counts = tile_count.astype(f32)
    slots = lax.broadcasted_iota(jnp.int32, (TR, K), 1)
    scales = jnp.where(slots < tile_count[:, None], 1.0, 0.0) / jnp.sqrt(counts)[:, None]
    pos = jnp.stack([lax.axis_index("yh"), lax.axis_index(RING)]).astype(jnp.int32)
    shape = jax.ShapeDtypeStruct

    with jax.named_scope("gather_features"):
        mine = features.T.reshape(W, TR, T).transpose(1, 0, 2)
        far = lax.all_gather(mine, "zh")
        own = jnp.stack([far, across(far)])
        m, p = along(own, 1), along(own, -1)
        t0, t1 = along(own[0], 2), along(own[1], -2)
    weight_parts, tiles_hi, tiles_lo = call(
        prepare_kernel,
        (shape((2, F, F), bf16), shape((TR, T, K * T), bf16), shape((TR, T, K * T), bf16)),
        4 * F**3, 8 * 2**20, [SMEM, VMEM, pl.BlockSpec(memory_space=pl.ANY)],
        [pltpu.VMEM((TR, K, T, T), f32), pltpu.SemaphoreType.DMA((TR,))],
    )(scales, weight, tile_values)
    packed = call(
        gather_kernel, shape((C, 16, T), f32), 10**8, 6 * 2**20, [SMEM] * 2 + [VMEM] * 8,
        [pltpu.VMEM((32, TR, W, T), f32)],
    )(tile_cols, pos, own, p, t0, t1, m, tiles_hi, tiles_lo, cotangent.T)
    with jax.named_scope("to_nodes"):
        packed = lax.all_to_all(packed, COLS, 0, 0)
    layer = call(layer_kernel, shape((C, 16 + T, T), f32), 10**8, 3 * 2**20, [VMEM] * 2)(packed, weight_parts)
    with jax.named_scope("to_features"):
        layer = lax.all_to_all(layer, COLS, 0, 0)
    activated, parts = call(
        spread_kernel, (shape((W, TR * T), f32), shape((32, BLK, T), f32)), 10**8, 7 * 2**20,
        [SMEM] * 2 + [VMEM] * 3, [pltpu.VMEM((T, T), f32)],
    )(tile_cols, pos, layer, tiles_hi, tiles_lo)
    with jax.named_scope("add_blocks"):
        parts = parts.reshape(4, 2, 4, BLK, T)
        t1, m1, p1 = along(parts[2, 1], -2), along(parts[1, 1], 1), along(parts[3, 1], -1)
        t0, m0, p0 = along(parts[2, 0], 2), along(parts[1, 0], 1), along(parts[3, 0], -1)
        y1 = across(parts[0, 1] + t1 + m1 + p1)
        y0 = parts[0, 0] + t0 + m0 + p0 + y1
        half_up = along(y0[2, :64], 4)
        half_down = along(y0[2, 64:], -4)
        up = along(jnp.concatenate([y0[1, :64] + half_up, y0[1, 64:]]), 4)
        down = along(jnp.concatenate([y0[3, :64], y0[3, 64:] + half_down]), -4)
    grad_features, grad_weight = call(
        last_kernel, (shape((W, TR * T), f32), shape((16, W), f32)), 10**6, 2**19, [SMEM] + [VMEM] * 3,
    )(pos, y0[0], up, down)
    return activated.T, grad_features.T, grad_weight.T


def solution(mesh):
    grid = Mesh(mesh.devices.reshape(2, 4, 4, 2, 4, 2), ROWS + COLS)
    return jax.shard_map(
        local,
        mesh=grid,
        in_specs=(P(ROWS, COLS), P(), P(ROWS, None), P(ROWS), P(ROWS, None, None, None), P(ROWS, COLS)),
        out_specs=(P(ROWS, COLS), P(ROWS, COLS), P(COLS, ROWS)),
        check_vma=False,
    )
```

```python
import jax
import jax.numpy as jnp
from jax import lax
from jax.experimental import pallas as pl
from jax.experimental.pallas import tpu as pltpu
from jax.sharding import Mesh, PartitionSpec as P

ROWS = ("yh", "zh", "zl")
RING = ("zh", "zl")
COLS = ("yl", "x", "core")
F = 512
W = 32
T = 128
K = 12
TR = 4
C = 16
G = 4
BLK = TR * W + 8
f32, bf16 = jnp.float32, jnp.bfloat16
VMEM = pl.BlockSpec(memory_space=pltpu.VMEM)
SMEM = pl.BlockSpec(memory_space=pltpu.SMEM)
NT_DIMS = (((1,), (1,)), ((), ()))
NN_DIMS = (((1,), (0,)), ((), ()))
TN_DIMS = (((0,), (0,)), ((), ()))


def dot(a, b, dims=NN_DIMS):
    return lax.dot_general(a, b, dims, preferred_element_type=f32)


def split(x):
    hi = x.astype(bf16)
    return hi, (x - hi.astype(f32)).astype(bf16)


def call(kernel, outs, flops, moved, specs, scratch=(), grant=12):
    return pl.pallas_call(
        kernel,
        out_shape=outs,
        in_specs=specs,
        out_specs=jax.tree.map(lambda _: VMEM, outs),
        scratch_shapes=scratch,
        compiler_params=pltpu.CompilerParams(vmem_limit_bytes=grant * 2**20),
        cost_estimate=pl.CostEstimate(flops=flops, bytes_accessed=moved, transcendentals=0),
    )


def regroup(piece):
    return [jnp.concatenate([piece(g, k) for g in range(G)], 1) for k in range(4)]


def prepare_kernel(scale_ref, w_ref, tiles_ref, w_out, hi_out, lo_out, held, sems):
    copies = [pltpu.make_async_copy(tiles_ref.at[t], held.at[t], sems.at[t]) for t in range(TR)]
    for copy in copies:
        copy.start()
    rows = [w_ref[c * W + g * 8:c * W + g * 8 + 8, :] for g in range(G) for c in range(C)]
    hi, lo = split(jnp.concatenate(rows, 0))
    old = lax.broadcasted_iota(jnp.int32, (F, F), 0)
    new = lax.broadcasted_iota(jnp.int32, (F, F), 1)
    source = ((new // 8) % C) * W + (new // (8 * C)) * 8 + new % 8
    order = jnp.where(old == source, 1.0, 0.0).astype(bf16)
    w_out[0] = dot(hi, order).astype(bf16)
    w_out[1] = dot(lo, order).astype(bf16)
    for t in range(TR):
        copies[t].wait()
        for s in range(K):
            hi, lo = split(held[t, s] * scale_ref[t, s])
            hi_out[t, :, T * s:T * s + T] = hi
            lo_out[t, :, T * s:T * s + T] = lo


def near(pos_ref, col):
    return ((col // 4) % 4 - pos_ref[1] % 4 + 4) % 4, (col // 64 - pos_ref[0] + 2) % 2


def source_place(pos_ref, col):
    rel_q, rel_y = near(pos_ref, col)
    return rel_q * 8 + rel_y * 4 + (col // 16) % 4


def target_zh(z, rel_q, rel_y):
    by = jnp.where(rel_q == 3, -1, jnp.where(rel_q == 2, 2 - 4 * rel_y, rel_q))
    return (z + by + 16) % 16 // 4


def target_place(pos_ref, col):
    rel_q, rel_y = near(pos_ref, col)
    return rel_q * 8 + rel_y * 4 + ((col // 16) % 4 - target_zh(pos_ref[1], rel_q, rel_y) + 4) % 4


def gather_kernel(cols_ref, pos_ref, y_ref, p0, p1, t0, t1, m_ref, hi_ref, lo_ref, cot_ref, out_ref, held):
    for at, ref in ((0, y_ref), (8, p0), (12, p1), (16, t0), (20, t1), (24, m_ref)):
        for m in range(4):
            if len(ref.shape) == 4:
                held[at + m] = ref[m]
            else:
                for y in range(2):
                    held[at + 4 * y + m] = ref[y, m]
    for t in range(TR):
        picked = []
        for s in range(K):
            col = cols_ref[t, s]
            picked.append(held[source_place(pos_ref, col), col % 4])
        left_hi, left_lo = split(jnp.concatenate(picked, 1))
        both = dot(jnp.concatenate([left_hi, left_lo], 0), hi_ref[t], NT_DIMS)
        agg = both[:W] + both[W:] + dot(left_hi, lo_ref[t], NT_DIMS)
        parts = regroup(lambda g, k: agg[8 * g:8 * g + 8, W * k:W * k + W])
        cots = regroup(lambda g, k: cot_ref[8 * g:8 * g + 8, T * t + W * k:T * t + W * k + W])
        for k in range(4):
            out_ref[4 * t + k, 0:8, :] = parts[k]
            out_ref[4 * t + k, 8:16, :] = cots[k]


def node_rows(block):
    turned = block.reshape(T, T).T
    return jnp.concatenate([turned[W * g:W * g + W] for g in range(G)], 1)


def node_cols(rows):
    turned = jnp.concatenate([rows[:, T * g:T * g + T] for g in range(G)], 0)
    return turned.T.reshape(C, 8, T)


def layer_kernel(in_ref, w_ref, out_ref):
    agg = node_rows(in_ref[:, 0:8, :])
    cot = node_rows(in_ref[:, 8:16, :])
    agg_hi, agg_lo = split(agg)
    both = dot(jnp.concatenate([agg_hi, agg_lo], 0), w_ref[0])
    pre = both[:W] + both[W:] + dot(agg_hi, w_ref[1])
    sig = jax.nn.sigmoid(pre)
    act = pre * sig
    grad = cot * (sig + act * (1.0 - sig))
    grad_hi, grad_lo = split(grad)
    both = dot(jnp.concatenate([grad_hi, grad_lo], 0), w_ref[0], NT_DIMS)
    back = both[:W] + both[W:] + dot(grad_hi, w_ref[1], NT_DIMS)
    out_ref[:, 0:8, :] = node_cols(back)
    out_ref[:, 8:16, :] = node_cols(act)
    left = jnp.concatenate([agg_hi, agg_lo, agg_hi], 0)
    right = jnp.concatenate([grad_hi, grad_hi, grad_lo], 0)
    for g in range(G):
        part = dot(left[:, T * g:T * g + T], right, TN_DIMS)
        for h in range(4):
            at = 16 + (4 * g + h) * 8
            out_ref[:, at:at + 8, :] = part[:, T * h:T * h + T].reshape(C, 8, T)


def spread_kernel(cols_ref, pos_ref, in_ref, hi_ref, lo_ref, act_ref, out_ref, weight_part):
    yh, z = pos_ref[0], pos_ref[1]
    total = in_ref[0, 16:16 + T, :]
    for c in range(1, C):
        total = total + in_ref[c, 16:16 + T, :]
    weight_part[...] = total.T
    out_ref[:, 0:TR * W, :] = jnp.zeros((32, TR * W, T), f32)
    for q in range(4):
        for y in range(2):
            for m in range(4):
                far = (m + target_zh(z, q, y)) % 4
                block = ((yh + y) % 2) * 16 + far * 4 + (z + q) % 4
                start = pl.multiple_of((block // 2) * 8, 8)
                out_ref[q * 8 + y * 4 + m, TR * W:BLK, :] = weight_part[pl.ds(start, 8), :]
    for t in range(TR):
        grad = regroup(lambda k, g: in_ref[4 * t + k, 0:8, W * g:W * g + W])
        act = regroup(lambda k, g: in_ref[4 * t + k, 8:16, W * g:W * g + W])
        act_ref[:, T * t:T * t + T] = jnp.concatenate(act, 0)
        grad_hi, grad_lo = split(jnp.concatenate(grad, 0))
        both = dot(jnp.concatenate([grad_hi, grad_lo], 0), hi_ref[t])
        sent = both[:W] + both[W:] + dot(grad_hi, lo_ref[t])
        for s in range(K):
            col = cols_ref[t, s]
            block = target_place(pos_ref, col)
            at = pl.ds(pl.multiple_of((col % 4) * W, W), W)
            out_ref[block, at, :] = out_ref[block, at, :] + sent[:, T * s:T * s + T]


def last_kernel(pos_ref, own_ref, up_ref, down_ref, grad_ref, weight_ref):
    total = own_ref[...] + up_ref[...] + down_ref[...]
    for t in range(TR):
        grad_ref[:, T * t:T * t + T] = total[W * t:W * t + W]
    piece = total[TR * W:BLK]
    odd = jnp.concatenate([piece[:, 16:], piece[:, :16]], 1)
    piece = jnp.where(pos_ref[1] % 2 == 1, odd, piece)
    for h in range(2):
        cut = [piece[:, W * g + 8 * h:W * g + 8 * h + 8] for g in range(G)]
        weight_ref[8 * h:8 * h + 8, :] = jnp.concatenate(cut, 1)


def shift(size, by):
    return [(i, (i + by) % size) for i in range(size)]


def along(x, by):
    return lax.ppermute(x, RING, shift(16, by))


def across(x):
    return lax.ppermute(x, "yh", shift(2, 1))


def local(features, weight, tile_cols, tile_count, tile_values, cotangent):
    counts = tile_count.astype(f32)
    slots = lax.broadcasted_iota(jnp.int32, (TR, K), 1)
    scales = jnp.where(slots < tile_count[:, None], 1.0, 0.0) / jnp.sqrt(counts)[:, None]
    pos = jnp.stack([lax.axis_index("yh"), lax.axis_index(RING)]).astype(jnp.int32)
    shape = jax.ShapeDtypeStruct

    with jax.named_scope("gather_features"):
        mine = features.T.reshape(W, TR, T).transpose(1, 0, 2)
        far = lax.all_gather(mine, "zh")
        other = across(far)
        t0, p0 = along(far, 2), along(far, -1)
        t1, p1 = along(other, -2), along(other, -1)
        own = jnp.stack([far, other])
        m = along(own, 1)
    weight_parts, tiles_hi, tiles_lo = call(
        prepare_kernel,
        (shape((2, F, F), bf16), shape((TR, T, K * T), bf16), shape((TR, T, K * T), bf16)),
        4 * F**3, 8 * 2**20, [SMEM, VMEM, pl.BlockSpec(memory_space=pl.ANY)],
        [pltpu.VMEM((TR, K, T, T), f32), pltpu.SemaphoreType.DMA((TR,))],
    )(scales, weight, tile_values)
    packed = call(
        gather_kernel, shape((C, 16, T), f32), 10**8, 6 * 2**20, [SMEM] * 2 + [VMEM] * 9,
        [pltpu.VMEM((32, TR, W, T), f32)],
    )(tile_cols, pos, own, p0, p1, t0, t1, m, tiles_hi, tiles_lo, cotangent.T)
    with jax.named_scope("to_nodes"):
        packed = lax.all_to_all(packed, COLS, 0, 0)
    layer = call(layer_kernel, shape((C, 16 + T, T), f32), 10**8, 3 * 2**20, [VMEM] * 2)(packed, weight_parts)
    with jax.named_scope("to_features"):
        layer = lax.all_to_all(layer, COLS, 0, 0)
    activated, parts = call(
        spread_kernel, (shape((W, TR * T), f32), shape((32, BLK, T), f32)), 10**8, 7 * 2**20,
        [SMEM] * 2 + [VMEM] * 3, [pltpu.VMEM((T, T), f32)],
    )(tile_cols, pos, layer, tiles_hi, tiles_lo)
    with jax.named_scope("add_blocks"):
        parts = parts.reshape(4, 2, 4, BLK, T)
        t1, p1 = along(parts[2, 1], -2), along(parts[3, 1], -1)
        m, t0 = along(parts[1], 1), along(parts[2, 0], 2)
        other = parts[0, 1] + t1 + p1 + m[1]
        p0 = along(parts[3, 0] + other[0, 0, 0] * 0.0, -1)
        y0 = parts[0, 0] + t0 + m[0] + p0 + across(other)
        down = along(y0[3], -4)
        up = along(y0[1] + along(y0[2], 4), 4)
    grad_features, grad_weight = call(
        last_kernel, (shape((W, TR * T), f32), shape((16, W), f32)), 10**6, 2**19, [SMEM] + [VMEM] * 3,
    )(pos, y0[0], up, down)
    return activated.T, grad_features.T, grad_weight.T


def solution(mesh):
    grid = Mesh(mesh.devices.reshape(2, 4, 4, 2, 4, 2), ROWS + COLS)
    return jax.shard_map(
        local,
        mesh=grid,
        in_specs=(P(ROWS, COLS), P(), P(ROWS, None), P(ROWS), P(ROWS, None, None, None), P(ROWS, COLS)),
        out_specs=(P(ROWS, COLS), P(ROWS, COLS), P(COLS, ROWS)),
        check_vma=False,
    )
```

```python
import jax
import jax.numpy as jnp
from jax import lax
from jax.experimental import pallas as pl
from jax.experimental.pallas import tpu as pltpu
from jax.sharding import Mesh, PartitionSpec as P

ROWS = ("yh", "zh", "zl")
RING = ("zh", "zl")
COLS = ("yl", "x", "core")
F = 512
W = 32
T = 128
K = 12
TR = 4
C = 16
G = 4
BLK = TR * W + 8
f32, bf16 = jnp.float32, jnp.bfloat16
VMEM = pl.BlockSpec(memory_space=pltpu.VMEM)
SMEM = pl.BlockSpec(memory_space=pltpu.SMEM)
NT_DIMS = (((1,), (1,)), ((), ()))
NN_DIMS = (((1,), (0,)), ((), ()))
TN_DIMS = (((0,), (0,)), ((), ()))


def dot(a, b, dims=NN_DIMS):
    return lax.dot_general(a, b, dims, preferred_element_type=f32)


def split(x):
    hi = x.astype(bf16)
    return hi, (x - hi.astype(f32)).astype(bf16)


def call(kernel, outs, flops, moved, specs, scratch=(), grant=12):
    return pl.pallas_call(
        kernel,
        out_shape=outs,
        in_specs=specs,
        out_specs=jax.tree.map(lambda _: VMEM, outs),
        scratch_shapes=scratch,
        compiler_params=pltpu.CompilerParams(vmem_limit_bytes=grant * 2**20),
        cost_estimate=pl.CostEstimate(flops=flops, bytes_accessed=moved, transcendentals=0),
    )


def regroup(piece):
    return [jnp.concatenate([piece(g, k) for g in range(G)], 1) for k in range(4)]


def prepare_kernel(scale_ref, w_ref, tiles_ref, w_out, hi_out, lo_out, held, sems):
    copies = [pltpu.make_async_copy(tiles_ref.at[t], held.at[t], sems.at[t]) for t in range(TR)]
    for copy in copies:
        copy.start()
    rows = [w_ref[c * W + g * 8:c * W + g * 8 + 8, :] for g in range(G) for c in range(C)]
    hi, lo = split(jnp.concatenate(rows, 0))
    old = lax.broadcasted_iota(jnp.int32, (F, F), 0)
    new = lax.broadcasted_iota(jnp.int32, (F, F), 1)
    source = ((new // 8) % C) * W + (new // (8 * C)) * 8 + new % 8
    order = jnp.where(old == source, 1.0, 0.0).astype(bf16)
    w_out[0] = dot(hi, order).astype(bf16)
    w_out[1] = dot(lo, order).astype(bf16)
    for t in range(TR):
        copies[t].wait()
        for s in range(K):
            hi, lo = split(held[t, s] * scale_ref[t, s])
            hi_out[t, :, T * s:T * s + T] = hi
            lo_out[t, :, T * s:T * s + T] = lo


def near(pos_ref, col):
    return ((col // 4) % 4 - pos_ref[1] % 4 + 4) % 4, (col // 64 - pos_ref[0] + 2) % 2


def source_place(pos_ref, col):
    rel_q, rel_y = near(pos_ref, col)
    return rel_q * 8 + rel_y * 4 + (col // 16) % 4


def target_zh(z, rel_q, rel_y):
    by = jnp.where(rel_q == 3, -1, jnp.where(rel_q == 2, 2 - 4 * rel_y, rel_q))
    return (z + by + 16) % 16 // 4


def target_place(pos_ref, col):
    rel_q, rel_y = near(pos_ref, col)
    return rel_q * 8 + rel_y * 4 + ((col // 16) % 4 - target_zh(pos_ref[1], rel_q, rel_y) + 4) % 4


def gather_kernel(cols_ref, pos_ref, y_ref, p0, p1, t0, t1, m_ref, hi_ref, lo_ref, cot_ref, out_ref, held):
    for at, ref in ((0, y_ref), (8, p0), (12, p1), (16, t0), (20, t1), (24, m_ref)):
        for m in range(4):
            if len(ref.shape) == 4:
                held[at + m] = ref[m]
            else:
                for y in range(2):
                    held[at + 4 * y + m] = ref[y, m]
    for t in range(TR):
        picked = []
        for s in range(K):
            col = cols_ref[t, s]
            picked.append(held[source_place(pos_ref, col), col % 4])
        left_hi, left_lo = split(jnp.concatenate(picked, 1))
        both = dot(jnp.concatenate([left_hi, left_lo], 0), hi_ref[t], NT_DIMS)
        agg = both[:W] + both[W:] + dot(left_hi, lo_ref[t], NT_DIMS)
        parts = regroup(lambda g, k: agg[8 * g:8 * g + 8, W * k:W * k + W])
        cots = regroup(lambda g, k: cot_ref[8 * g:8 * g + 8, T * t + W * k:T * t + W * k + W])
        for k in range(4):
            out_ref[4 * t + k, 0:8, :] = parts[k]
            out_ref[4 * t + k, 8:16, :] = cots[k]


def node_rows(block):
    turned = block.reshape(T, T).T
    return jnp.concatenate([turned[W * g:W * g + W] for g in range(G)], 1)


def node_cols(rows):
    turned = jnp.concatenate([rows[:, T * g:T * g + T] for g in range(G)], 0)
    return turned.T.reshape(C, 8, T)


def layer_kernel(in_ref, w_ref, out_ref):
    agg = node_rows(in_ref[:, 0:8, :])
    cot = node_rows(in_ref[:, 8:16, :])
    agg_hi, agg_lo = split(agg)
    both = dot(jnp.concatenate([agg_hi, agg_lo], 0), w_ref[0])
    pre = both[:W] + both[W:] + dot(agg_hi, w_ref[1])
    sig = jax.nn.sigmoid(pre)
    act = pre * sig
    grad = cot * (sig + act * (1.0 - sig))
    grad_hi, grad_lo = split(grad)
    both = dot(jnp.concatenate([grad_hi, grad_lo], 0), w_ref[0], NT_DIMS)
    back = both[:W] + both[W:] + dot(grad_hi, w_ref[1], NT_DIMS)
    out_ref[:, 0:8, :] = node_cols(back)
    out_ref[:, 8:16, :] = node_cols(act)
    left = jnp.concatenate([agg_hi, agg_lo, agg_hi], 0)
    right = jnp.concatenate([grad_hi, grad_hi, grad_lo], 0)
    for g in range(G):
        part = dot(left[:, T * g:T * g + T], right, TN_DIMS)
        for h in range(4):
            at = 16 + (4 * g + h) * 8
            out_ref[:, at:at + 8, :] = part[:, T * h:T * h + T].reshape(C, 8, T)


def spread_kernel(cols_ref, pos_ref, in_ref, hi_ref, lo_ref, act_ref, out_ref, weight_part):
    yh, z = pos_ref[0], pos_ref[1]
    total = in_ref[0, 16:16 + T, :]
    for c in range(1, C):
        total = total + in_ref[c, 16:16 + T, :]
    weight_part[...] = total.T
    out_ref[:, 0:TR * W, :] = jnp.zeros((32, TR * W, T), f32)
    for q in range(4):
        for y in range(2):
            for m in range(4):
                far = (m + target_zh(z, q, y)) % 4
                block = ((yh + y) % 2) * 16 + far * 4 + (z + q) % 4
                start = pl.multiple_of((block // 2) * 8, 8)
                out_ref[q * 8 + y * 4 + m, TR * W:BLK, :] = weight_part[pl.ds(start, 8), :]
    for t in range(TR):
        grad = regroup(lambda k, g: in_ref[4 * t + k, 0:8, W * g:W * g + W])
        act = regroup(lambda k, g: in_ref[4 * t + k, 8:16, W * g:W * g + W])
        act_ref[:, T * t:T * t + T] = jnp.concatenate(act, 0)
        grad_hi, grad_lo = split(jnp.concatenate(grad, 0))
        both = dot(jnp.concatenate([grad_hi, grad_lo], 0), hi_ref[t])
        sent = both[:W] + both[W:] + dot(grad_hi, lo_ref[t])
        for s in range(K):
            col = cols_ref[t, s]
            block = target_place(pos_ref, col)
            at = pl.ds(pl.multiple_of((col % 4) * W, W), W)
            out_ref[block, at, :] = out_ref[block, at, :] + sent[:, T * s:T * s + T]


def last_kernel(pos_ref, own_ref, up_ref, down_ref, grad_ref, weight_ref):
    total = own_ref[...] + up_ref[...] + down_ref[...]
    for t in range(TR):
        grad_ref[:, T * t:T * t + T] = total[W * t:W * t + W]
    piece = total[TR * W:BLK]
    odd = jnp.concatenate([piece[:, 16:], piece[:, :16]], 1)
    piece = jnp.where(pos_ref[1] % 2 == 1, odd, piece)
    for h in range(2):
        cut = [piece[:, W * g + 8 * h:W * g + 8 * h + 8] for g in range(G)]
        weight_ref[8 * h:8 * h + 8, :] = jnp.concatenate(cut, 1)


def shift(size, by):
    return [(i, (i + by) % size) for i in range(size)]


def along(x, by):
    return lax.ppermute(x, RING, shift(16, by))


def across(x):
    return lax.ppermute(x, "yh", shift(2, 1))


def local(features, weight, tile_cols, tile_count, tile_values, cotangent):
    counts = tile_count.astype(f32)
    slots = lax.broadcasted_iota(jnp.int32, (TR, K), 1)
    scales = jnp.where(slots < tile_count[:, None], 1.0, 0.0) / jnp.sqrt(counts)[:, None]
    pos = jnp.stack([lax.axis_index("yh"), lax.axis_index(RING)]).astype(jnp.int32)
    shape = jax.ShapeDtypeStruct

    with jax.named_scope("gather_features"):
        mine = features.T.reshape(W, TR, T).transpose(1, 0, 2)
        far = lax.all_gather(mine, "zh")
        other = across(far)
        t0, p0 = along(far, 2), along(far, -1)
        t1, p1 = along(other, -2), along(other, -1)
        own = jnp.stack([far, other])
        m = along(own, 1)
    weight_parts, tiles_hi, tiles_lo = call(
        prepare_kernel,
        (shape((2, F, F), bf16), shape((TR, T, K * T), bf16), shape((TR, T, K * T), bf16)),
        4 * F**3, 8 * 2**20, [SMEM, VMEM, pl.BlockSpec(memory_space=pl.ANY)],
        [pltpu.VMEM((TR, K, T, T), f32), pltpu.SemaphoreType.DMA((TR,))],
    )(scales, weight, tile_values)
    packed = call(
        gather_kernel, shape((C, 16, T), f32), 10**8, 6 * 2**20, [SMEM] * 2 + [VMEM] * 9,
        [pltpu.VMEM((32, TR, W, T), f32)],
    )(tile_cols, pos, own, p0, p1, t0, t1, m, tiles_hi, tiles_lo, cotangent.T)
    with jax.named_scope("to_nodes"):
        packed = lax.all_to_all(packed, COLS, 0, 0)
    layer = call(layer_kernel, shape((C, 16 + T, T), f32), 10**8, 3 * 2**20, [VMEM] * 2)(packed, weight_parts)
    with jax.named_scope("to_features"):
        layer = lax.all_to_all(layer, COLS, 0, 0)
    activated, parts = call(
        spread_kernel, (shape((W, TR * T), f32), shape((32, BLK, T), f32)), 10**8, 7 * 2**20,
        [SMEM] * 2 + [VMEM] * 3, [pltpu.VMEM((T, T), f32)],
    )(tile_cols, pos, layer, tiles_hi, tiles_lo)
    with jax.named_scope("add_blocks"):
        parts = parts.reshape(4, 2, 4, BLK, T)
        t1, m1, p1 = along(parts[2, 1], -2), along(parts[1, 1], 1), along(parts[3, 1], -1)
        t0, m0, p0 = along(parts[2, 0], 2), along(parts[1, 0], 1), along(parts[3, 0], -1)
        y1 = across(parts[0, 1] + t1 + m1 + p1)
        y0 = parts[0, 0] + t0 + m0 + p0 + y1
        down = along(y0[3], -4)
        up = along(y0[1] + along(y0[2], 4), 4)
    grad_features, grad_weight = call(
        last_kernel, (shape((W, TR * T), f32), shape((16, W), f32)), 10**6, 2**19, [SMEM] + [VMEM] * 3,
    )(pos, y0[0], up, down)
    return activated.T, grad_features.T, grad_weight.T


def solution(mesh):
    grid = Mesh(mesh.devices.reshape(2, 4, 4, 2, 4, 2), ROWS + COLS)
    return jax.shard_map(
        local,
        mesh=grid,
        in_specs=(P(ROWS, COLS), P(), P(ROWS, None), P(ROWS), P(ROWS, None, None, None), P(ROWS, COLS)),
        out_specs=(P(ROWS, COLS), P(ROWS, COLS), P(COLS, ROWS)),
        check_vma=False,
    )
```

```python
import jax
import jax.numpy as jnp
from jax import lax
from jax.experimental import pallas as pl
from jax.experimental.pallas import tpu as pltpu
from jax.sharding import Mesh, PartitionSpec as P

ROWS = ("yh", "zh", "zl")
RING = ("zh", "zl")
COLS = ("yl", "x", "core")
F = 512
W = 32
T = 128
K = 12
TR = 4
C = 16
G = 4
BLK = TR * W + 8
f32, bf16 = jnp.float32, jnp.bfloat16
VMEM = pl.BlockSpec(memory_space=pltpu.VMEM)
SMEM = pl.BlockSpec(memory_space=pltpu.SMEM)
NT_DIMS = (((1,), (1,)), ((), ()))
NN_DIMS = (((1,), (0,)), ((), ()))
TN_DIMS = (((0,), (0,)), ((), ()))


def dot(a, b, dims=NN_DIMS):
    return lax.dot_general(a, b, dims, preferred_element_type=f32)


def split(x):
    hi = x.astype(bf16)
    return hi, (x - hi.astype(f32)).astype(bf16)


def call(kernel, outs, flops, moved, specs, scratch=(), grant=12):
    return pl.pallas_call(
        kernel,
        out_shape=outs,
        in_specs=specs,
        out_specs=jax.tree.map(lambda _: VMEM, outs),
        scratch_shapes=scratch,
        compiler_params=pltpu.CompilerParams(vmem_limit_bytes=grant * 2**20),
        cost_estimate=pl.CostEstimate(flops=flops, bytes_accessed=moved, transcendentals=0),
    )


def regroup(piece):
    return [jnp.concatenate([piece(g, k) for g in range(G)], 1) for k in range(4)]


def prepare_kernel(scale_ref, w_ref, tiles_ref, w_out, hi_out, lo_out, held, sems):
    copies = [pltpu.make_async_copy(tiles_ref.at[t], held.at[t], sems.at[t]) for t in range(TR)]
    for copy in copies:
        copy.start()
    rows = [w_ref[c * W + g * 8:c * W + g * 8 + 8, :] for g in range(G) for c in range(C)]
    hi, lo = split(jnp.concatenate(rows, 0))
    old = lax.broadcasted_iota(jnp.int32, (F, F), 0)
    new = lax.broadcasted_iota(jnp.int32, (F, F), 1)
    source = ((new // 8) % C) * W + (new // (8 * C)) * 8 + new % 8
    order = jnp.where(old == source, 1.0, 0.0).astype(bf16)
    w_out[0] = dot(hi, order).astype(bf16)
    w_out[1] = dot(lo, order).astype(bf16)
    for t in range(TR):
        copies[t].wait()
        for s in range(K):
            hi, lo = split(held[t, s] * scale_ref[t, s])
            hi_out[t, :, T * s:T * s + T] = hi
            lo_out[t, :, T * s:T * s + T] = lo


def near(pos_ref, col):
    return ((col // 4) % 4 - pos_ref[1] % 4 + 4) % 4, (col // 64 - pos_ref[0] + 2) % 2


def source_place(pos_ref, col):
    rel_q, rel_y = near(pos_ref, col)
    return rel_q * 8 + rel_y * 4 + (col // 16) % 4


def target_zh(z, rel_q, rel_y):
    by = jnp.where(rel_q == 3, -1, jnp.where(rel_q == 2, 2 - 4 * rel_y, rel_q))
    return (z + by + 16) % 16 // 4


def target_place(pos_ref, col):
    rel_q, rel_y = near(pos_ref, col)
    return rel_q * 8 + rel_y * 4 + ((col // 16) % 4 - target_zh(pos_ref[1], rel_q, rel_y) + 4) % 4


def gather_kernel(cols_ref, pos_ref, y0, y1, p0, p1, t0, t1, m0, m1, hi_ref, lo_ref, cot_ref, out_ref, held):
    for at, ref in enumerate((y0, y1, p0, p1, t0, t1, m0, m1)):
        for m in range(4):
            for t in range(TR):
                held[4 * at + m, t] = ref[m, :, T * t:T * t + T]
    for t in range(TR):
        picked = []
        for s in range(K):
            col = cols_ref[t, s]
            picked.append(held[source_place(pos_ref, col), col % 4])
        left_hi, left_lo = split(jnp.concatenate(picked, 1))
        both = dot(jnp.concatenate([left_hi, left_lo], 0), hi_ref[t], NT_DIMS)
        agg = both[:W] + both[W:] + dot(left_hi, lo_ref[t], NT_DIMS)
        parts = regroup(lambda g, k: agg[8 * g:8 * g + 8, W * k:W * k + W])
        cots = regroup(lambda g, k: cot_ref[8 * g:8 * g + 8, T * t + W * k:T * t + W * k + W])
        for k in range(4):
            out_ref[4 * t + k, 0:8, :] = parts[k]
            out_ref[4 * t + k, 8:16, :] = cots[k]


def node_rows(block):
    turned = block.reshape(T, T).T
    return jnp.concatenate([turned[W * g:W * g + W] for g in range(G)], 1)


def node_cols(rows):
    turned = jnp.concatenate([rows[:, T * g:T * g + T] for g in range(G)], 0)
    return turned.T.reshape(C, 8, T)


def layer_kernel(in_ref, w_ref, out_ref):
    agg = node_rows(in_ref[:, 0:8, :])
    cot = node_rows(in_ref[:, 8:16, :])
    agg_hi, agg_lo = split(agg)
    both = dot(jnp.concatenate([agg_hi, agg_lo], 0), w_ref[0])
    pre = both[:W] + both[W:] + dot(agg_hi, w_ref[1])
    sig = jax.nn.sigmoid(pre)
    act = pre * sig
    grad = cot * (sig + act * (1.0 - sig))
    grad_hi, grad_lo = split(grad)
    both = dot(jnp.concatenate([grad_hi, grad_lo], 0), w_ref[0], NT_DIMS)
    back = both[:W] + both[W:] + dot(grad_hi, w_ref[1], NT_DIMS)
    out_ref[:, 0:8, :] = node_cols(back)
    out_ref[:, 8:16, :] = node_cols(act)
    left = jnp.concatenate([agg_hi, agg_lo, agg_hi], 0)
    right = jnp.concatenate([grad_hi, grad_hi, grad_lo], 0)
    for g in range(G):
        part = dot(left[:, T * g:T * g + T], right, TN_DIMS)
        for h in range(4):
            at = 16 + (4 * g + h) * 8
            out_ref[:, at:at + 8, :] = part[:, T * h:T * h + T].reshape(C, 8, T)


def spread_kernel(cols_ref, pos_ref, in_ref, hi_ref, lo_ref, act_ref, out_ref, weight_part):
    yh, z = pos_ref[0], pos_ref[1]
    total = in_ref[0, 16:16 + T, :]
    for c in range(1, C):
        total = total + in_ref[c, 16:16 + T, :]
    weight_part[...] = total.T
    out_ref[:, 0:TR * W, :] = jnp.zeros((32, TR * W, T), f32)
    for q in range(4):
        for y in range(2):
            for m in range(4):
                far = (m + target_zh(z, q, y)) % 4
                block = ((yh + y) % 2) * 16 + far * 4 + (z + q) % 4
                start = pl.multiple_of((block // 2) * 8, 8)
                out_ref[q * 8 + y * 4 + m, TR * W:BLK, :] = weight_part[pl.ds(start, 8), :]
    for t in range(TR):
        grad = regroup(lambda k, g: in_ref[4 * t + k, 0:8, W * g:W * g + W])
        act = regroup(lambda k, g: in_ref[4 * t + k, 8:16, W * g:W * g + W])
        act_ref[:, T * t:T * t + T] = jnp.concatenate(act, 0)
        grad_hi, grad_lo = split(jnp.concatenate(grad, 0))
        both = dot(jnp.concatenate([grad_hi, grad_lo], 0), hi_ref[t])
        sent = both[:W] + both[W:] + dot(grad_hi, lo_ref[t])
        for s in range(K):
            col = cols_ref[t, s]
            block = target_place(pos_ref, col)
            at = pl.ds(pl.multiple_of((col % 4) * W, W), W)
            out_ref[block, at, :] = out_ref[block, at, :] + sent[:, T * s:T * s + T]


def last_kernel(pos_ref, own_ref, up_ref, down_ref, grad_ref, weight_ref):
    total = own_ref[...] + up_ref[...] + down_ref[...]
    for t in range(TR):
        grad_ref[:, T * t:T * t + T] = total[W * t:W * t + W]
    piece = total[TR * W:BLK]
    odd = jnp.concatenate([piece[:, 16:], piece[:, :16]], 1)
    piece = jnp.where(pos_ref[1] % 2 == 1, odd, piece)
    for h in range(2):
        cut = [piece[:, W * g + 8 * h:W * g + 8 * h + 8] for g in range(G)]
        weight_ref[8 * h:8 * h + 8, :] = jnp.concatenate(cut, 1)


def shift(size, by):
    return [(i, (i + by) % size) for i in range(size)]


def along(x, by):
    return lax.ppermute(x, RING, shift(16, by))


def across(x):
    return lax.ppermute(x, "yh", shift(2, 1))


def local(features, weight, tile_cols, tile_count, tile_values, cotangent):
    counts = tile_count.astype(f32)
    slots = lax.broadcasted_iota(jnp.int32, (TR, K), 1)
    scales = jnp.where(slots < tile_count[:, None], 1.0, 0.0) / jnp.sqrt(counts)[:, None]
    pos = jnp.stack([lax.axis_index("yh"), lax.axis_index(RING)]).astype(jnp.int32)
    shape = jax.ShapeDtypeStruct

    with jax.named_scope("gather_features"):
        far = lax.all_gather(features.T, "zh")
        other = across(far)
        m0, p0 = along(far, 1), along(far, -1)
        p1, m1 = along(other, -1), along(other, 1)
        t0, t1 = along(m0, 1), along(p1, -1)
    weight_parts, tiles_hi, tiles_lo = call(
        prepare_kernel,
        (shape((2, F, F), bf16), shape((TR, T, K * T), bf16), shape((TR, T, K * T), bf16)),
        4 * F**3, 8 * 2**20, [SMEM, VMEM, pl.BlockSpec(memory_space=pl.ANY)],
        [pltpu.VMEM((TR, K, T, T), f32), pltpu.SemaphoreType.DMA((TR,))],
    )(scales, weight, tile_values)
    packed = call(
        gather_kernel, shape((C, 16, T), f32), 10**8, 6 * 2**20, [SMEM] * 2 + [VMEM] * 11,
        [pltpu.VMEM((32, TR, W, T), f32)],
    )(tile_cols, pos, far, other, p0, p1, t0, t1, m0, m1, tiles_hi, tiles_lo, cotangent.T)
    with jax.named_scope("to_nodes"):
        packed = lax.all_to_all(packed, COLS, 0, 0)
    layer = call(layer_kernel, shape((C, 16 + T, T), f32), 10**8, 3 * 2**20, [VMEM] * 2)(packed, weight_parts)
    with jax.named_scope("to_features"):
        layer = lax.all_to_all(layer, COLS, 0, 0)
    activated, parts = call(
        spread_kernel, (shape((W, TR * T), f32), shape((32, BLK, T), f32)), 10**8, 7 * 2**20,
        [SMEM] * 2 + [VMEM] * 3, [pltpu.VMEM((T, T), f32)],
    )(tile_cols, pos, layer, tiles_hi, tiles_lo)
    with jax.named_scope("add_blocks"):
        parts = parts.reshape(4, 2, 4, BLK, T)
        t1, t0 = along(parts[2, 1], -1), along(parts[2, 0], 1)
        m1, p1 = along(parts[1, 1], 1), along(parts[3, 1] + t1, -1)
        p0, m0 = along(parts[3, 0], -1), along(parts[1, 0] + t0, 1)
        y1 = across(parts[0, 1] + m1 + p1)
        y0 = parts[0, 0] + m0 + p0 + y1
        down = along(y0[3], -4)
        up = along(y0[1] + along(y0[2], 4), 4)
    grad_features, grad_weight = call(
        last_kernel, (shape((W, TR * T), f32), shape((16, W), f32)), 10**6, 2**19, [SMEM] + [VMEM] * 3,
    )(pos, y0[0], up, down)
    return activated.T, grad_features.T, grad_weight.T


def solution(mesh):
    grid = Mesh(mesh.devices.reshape(2, 4, 4, 2, 4, 2), ROWS + COLS)
    return jax.shard_map(
        local,
        mesh=grid,
        in_specs=(P(ROWS, COLS), P(), P(ROWS, None), P(ROWS), P(ROWS, None, None, None), P(ROWS, COLS)),
        out_specs=(P(ROWS, COLS), P(ROWS, COLS), P(COLS, ROWS)),
        check_vma=False,
    )
```

```python
import functools

import jax
import jax.numpy as jnp
from jax import lax
from jax.experimental import pallas as pl
from jax.experimental.pallas import tpu as pltpu
from jax.sharding import Mesh, PartitionSpec as P

ROWS = ("yh", "zh", "zl")
RING = ("zh", "zl")
COLS = ("yl", "x", "core")
F = 512
W = 32
T = 128
K = 12
TR = 4
C = 16
G = 4
BLK = TR * W + 8
f32, bf16 = jnp.float32, jnp.bfloat16
VMEM = pl.BlockSpec(memory_space=pltpu.VMEM)
SMEM = pl.BlockSpec(memory_space=pltpu.SMEM)
NT_DIMS = (((1,), (1,)), ((), ()))
NN_DIMS = (((1,), (0,)), ((), ()))
TN_DIMS = (((0,), (0,)), ((), ()))


def dot(a, b, dims=NN_DIMS):
    return lax.dot_general(a, b, dims, preferred_element_type=f32)


def split(x):
    hi = x.astype(bf16)
    return hi, (x - hi.astype(f32)).astype(bf16)


def call(kernel, outs, flops, moved, specs, scratch=(), grant=12):
    return pl.pallas_call(
        kernel,
        out_shape=outs,
        in_specs=specs,
        out_specs=jax.tree.map(lambda _: VMEM, outs),
        scratch_shapes=scratch,
        compiler_params=pltpu.CompilerParams(vmem_limit_bytes=grant * 2**20),
        cost_estimate=pl.CostEstimate(flops=flops, bytes_accessed=moved, transcendentals=0),
    )


def regroup(piece):
    return [jnp.concatenate([piece(g, k) for g in range(G)], 1) for k in range(4)]


def prepare_kernel(count_ref, w_ref, tiles_ref, w_out, hi_out, lo_out):
    for t in range(TR):
        count = count_ref[t]
        scale = 1.0 / jnp.sqrt(jnp.full((T, T), count, jnp.int32).astype(f32))
        for s in range(K):
            hi, lo = split(tiles_ref[t, s] * jnp.where(s < count, scale, 0.0))
            hi_out[t, :, T * s:T * s + T] = hi
            lo_out[t, :, T * s:T * s + T] = lo
    rows = [w_ref[c * W + g * 8:c * W + g * 8 + 8, :] for g in range(G) for c in range(C)]
    hi, lo = split(jnp.concatenate(rows, 0))
    old = lax.broadcasted_iota(jnp.int32, (F, F), 0)
    new = lax.broadcasted_iota(jnp.int32, (F, F), 1)
    source = ((new // 8) % C) * W + (new // (8 * C)) * 8 + new % 8
    order = jnp.where(old == source, 1.0, 0.0).astype(bf16)
    w_out[0] = dot(hi, order).astype(bf16)
    w_out[1] = dot(lo, order).astype(bf16)


def add_kernel(at, parts_ref, passed_ref, out_ref):
    for m in range(4):
        out_ref[m] = parts_ref[at + m] + passed_ref[m]


def near(pos_ref, col):
    return ((col // 4) % 4 - pos_ref[1] % 4 + 4) % 4, (col // 64 - pos_ref[0] + 2) % 2


def source_place(pos_ref, col):
    rel_q, rel_y = near(pos_ref, col)
    return rel_q * 8 + rel_y * 4 + (col // 16) % 4


def target_zh(z, rel_q, rel_y):
    by = jnp.where(rel_q == 3, -1, jnp.where(rel_q == 2, 2 - 4 * rel_y, rel_q))
    return (z + by + 16) % 16 // 4


def target_place(pos_ref, col):
    rel_q, rel_y = near(pos_ref, col)
    return rel_q * 8 + rel_y * 4 + ((col // 16) % 4 - target_zh(pos_ref[1], rel_q, rel_y) + 4) % 4


def gather_kernel(cols_ref, pos_ref, y0, y1, p0, p1, t0, t1, m0, m1, hi_ref, lo_ref, cot_ref, out_ref, held):
    for at, ref in enumerate((y0, y1, p0, p1, t0, t1, m0, m1)):
        for m in range(4):
            for t in range(TR):
                held[4 * at + m, t] = ref[m, :, T * t:T * t + T]
    for t in range(TR):
        picked = []
        for s in range(K):
            col = cols_ref[t, s]
            picked.append(held[source_place(pos_ref, col), col % 4])
        left_hi, left_lo = split(jnp.concatenate(picked, 1))
        both = dot(jnp.concatenate([left_hi, left_lo], 0), hi_ref[t], NT_DIMS)
        agg = both[:W] + both[W:] + dot(left_hi, lo_ref[t], NT_DIMS)
        parts = regroup(lambda g, k: agg[8 * g:8 * g + 8, W * k:W * k + W])
        cots = regroup(lambda g, k: cot_ref[8 * g:8 * g + 8, T * t + W * k:T * t + W * k + W])
        for k in range(4):
            out_ref[4 * t + k, 0:8, :] = parts[k]
            out_ref[4 * t + k, 8:16, :] = cots[k]


def node_rows(block):
    turned = block.reshape(T, T).T
    return jnp.concatenate([turned[W * g:W * g + W] for g in range(G)], 1)


def node_cols(rows):
    turned = jnp.concatenate([rows[:, T * g:T * g + T] for g in range(G)], 0)
    return turned.T.reshape(C, 8, T)


def layer_kernel(in_ref, w_ref, out_ref):
    agg = node_rows(in_ref[:, 0:8, :])
    cot = node_rows(in_ref[:, 8:16, :])
    agg_hi, agg_lo = split(agg)
    both = dot(jnp.concatenate([agg_hi, agg_lo], 0), w_ref[0])
    pre = both[:W] + both[W:] + dot(agg_hi, w_ref[1])
    sig = jax.nn.sigmoid(pre)
    act = pre * sig
    grad = cot * (sig + act * (1.0 - sig))
    grad_hi, grad_lo = split(grad)
    both = dot(jnp.concatenate([grad_hi, grad_lo], 0), w_ref[0], NT_DIMS)
    back = both[:W] + both[W:] + dot(grad_hi, w_ref[1], NT_DIMS)
    out_ref[:, 0:8, :] = node_cols(back)
    out_ref[:, 8:16, :] = node_cols(act)
    left = jnp.concatenate([agg_hi, agg_lo, agg_hi], 0)
    right = jnp.concatenate([grad_hi, grad_hi, grad_lo], 0)
    for g in range(G):
        part = dot(left[:, T * g:T * g + T], right, TN_DIMS)
        for h in range(4):
            at = 16 + (4 * g + h) * 8
            out_ref[:, at:at + 8, :] = part[:, T * h:T * h + T].reshape(C, 8, T)


def spread_kernel(cols_ref, pos_ref, in_ref, hi_ref, lo_ref, act_ref, out_ref, weight_part):
    yh, z = pos_ref[0], pos_ref[1]
    total = in_ref[0, 16:16 + T, :]
    for c in range(1, C):
        total = total + in_ref[c, 16:16 + T, :]
    weight_part[...] = total.T
    out_ref[:, 0:TR * W, :] = jnp.zeros((32, TR * W, T), f32)
    for q in range(4):
        for y in range(2):
            for m in range(4):
                far = (m + target_zh(z, q, y)) % 4
                block = ((yh + y) % 2) * 16 + far * 4 + (z + q) % 4
                start = pl.multiple_of((block // 2) * 8, 8)
                out_ref[q * 8 + y * 4 + m, TR * W:BLK, :] = weight_part[pl.ds(start, 8), :]
    for t in range(TR):
        grad = regroup(lambda k, g: in_ref[4 * t + k, 0:8, W * g:W * g + W])
        act = regroup(lambda k, g: in_ref[4 * t + k, 8:16, W * g:W * g + W])
        act_ref[:, T * t:T * t + T] = jnp.concatenate(act, 0)
        grad_hi, grad_lo = split(jnp.concatenate(grad, 0))
        both = dot(jnp.concatenate([grad_hi, grad_lo], 0), hi_ref[t])
        sent = both[:W] + both[W:] + dot(grad_hi, lo_ref[t])
        for s in range(K):
            col = cols_ref[t, s]
            block = target_place(pos_ref, col)
            at = pl.ds(pl.multiple_of((col % 4) * W, W), W)
            out_ref[block, at, :] = out_ref[block, at, :] + sent[:, T * s:T * s + T]


def last_kernel(pos_ref, own_ref, up_ref, down_ref, grad_ref, weight_ref):
    total = own_ref[...] + up_ref[...] + down_ref[...]
    for t in range(TR):
        grad_ref[:, T * t:T * t + T] = total[W * t:W * t + W]
    piece = total[TR * W:BLK]
    odd = jnp.concatenate([piece[:, 16:], piece[:, :16]], 1)
    piece = jnp.where(pos_ref[1] % 2 == 1, odd, piece)
    for h in range(2):
        cut = [piece[:, W * g + 8 * h:W * g + 8 * h + 8] for g in range(G)]
        weight_ref[8 * h:8 * h + 8, :] = jnp.concatenate(cut, 1)


def shift(size, by):
    return [(i, (i + by) % size) for i in range(size)]


def along(x, by):
    return lax.ppermute(x, RING, shift(16, by))


def across(x):
    return lax.ppermute(x, "yh", shift(2, 1))


def local(features, weight, tile_cols, tile_count, tile_values, cotangent):
    pos = jnp.stack([lax.axis_index("yh"), lax.axis_index(RING)]).astype(jnp.int32)
    shape = jax.ShapeDtypeStruct

    with jax.named_scope("gather_features"):
        far = lax.all_gather(features.T, "zh")
        other = across(far)
        m0, p0 = along(far, 1), along(far, -1)
        p1, m1 = along(other, -1), along(other, 1)
        t0, t1 = along(m0, 1), along(p1, -1)
    weight_parts, tiles_hi, tiles_lo = call(
        prepare_kernel,
        (shape((2, F, F), bf16), shape((TR, T, K * T), bf16), shape((TR, T, K * T), bf16)),
        4 * F**3, 8 * 2**20, [SMEM, VMEM, VMEM],
    )(tile_count, weight, tile_values)
    packed = call(
        gather_kernel, shape((C, 16, T), f32), 10**8, 6 * 2**20, [SMEM] * 2 + [VMEM] * 11,
        [pltpu.VMEM((32, TR, W, T), f32)],
    )(tile_cols, pos, far, other, p0, p1, t0, t1, m0, m1, tiles_hi, tiles_lo, cotangent.T)
    with jax.named_scope("to_nodes"):
        packed = lax.all_to_all(packed, COLS, 0, 0)
    layer = call(layer_kernel, shape((C, 16 + T, T), f32), 10**8, 3 * 2**20, [VMEM] * 2)(packed, weight_parts)
    with jax.named_scope("to_features"):
        layer = lax.all_to_all(layer, COLS, 0, 0)
    activated, parts = call(
        spread_kernel, (shape((W, TR * T), f32), shape((32, BLK, T), f32)), 10**8, 7 * 2**20,
        [SMEM] * 2 + [VMEM] * 3, [pltpu.VMEM((T, T), f32)],
    )(tile_cols, pos, layer, tiles_hi, tiles_lo)
    with jax.named_scope("add_blocks"):
        flat, parts = parts, parts.reshape(4, 2, 4, BLK, T)
        t1, t0 = along(parts[2, 1], -1), along(parts[2, 0], 1)
        m1 = along(parts[1, 1], 1)
        add = lambda at, passed: call(
            functools.partial(add_kernel, at), shape((4, BLK, T), f32), 10**5, 2**20, [VMEM] * 2, grant=4
        )(flat, passed)
        p1 = along(add(28, t1), -1)
        p0, m0 = along(parts[3, 0], -1), along(add(8, t0), 1)
        y1 = across(parts[0, 1] + m1 + p1)
        y0 = parts[0, 0] + m0 + p0 + y1
        down = along(y0[3], -4)
        up = along(y0[1] + along(y0[2], 4), 4)
    grad_features, grad_weight = call(
        last_kernel, (shape((W, TR * T), f32), shape((16, W), f32)), 10**6, 2**19, [SMEM] + [VMEM] * 3,
    )(pos, y0[0], up, down)
    return activated.T, grad_features.T, grad_weight.T


def solution(mesh):
    grid = Mesh(mesh.devices.reshape(2, 4, 4, 2, 4, 2), ROWS + COLS)
    return jax.shard_map(
        local,
        mesh=grid,
        in_specs=(P(ROWS, COLS), P(), P(ROWS, None), P(ROWS), P(ROWS, None, None, None), P(ROWS, COLS)),
        out_specs=(P(ROWS, COLS), P(ROWS, COLS), P(COLS, ROWS)),
        check_vma=False,
    )
```

```python
import functools

import jax
import jax.numpy as jnp
from jax import lax
from jax.experimental import pallas as pl
from jax.experimental.pallas import tpu as pltpu
from jax.sharding import Mesh, PartitionSpec as P

ROWS = ("yh", "zh", "zl")
RING = ("zh", "zl")
COLS = ("yl", "x", "core")
F = 512
W = 32
T = 128
K = 12
TR = 4
C = 16
G = 4
BLK = TR * W + 8
f32, bf16 = jnp.float32, jnp.bfloat16
VMEM = pl.BlockSpec(memory_space=pltpu.VMEM)
SMEM = pl.BlockSpec(memory_space=pltpu.SMEM)
NT_DIMS = (((1,), (1,)), ((), ()))
NN_DIMS = (((1,), (0,)), ((), ()))
TN_DIMS = (((0,), (0,)), ((), ()))


def dot(a, b, dims=NN_DIMS):
    return lax.dot_general(a, b, dims, preferred_element_type=f32)


def split(x):
    hi = x.astype(bf16)
    return hi, (x - hi.astype(f32)).astype(bf16)


def call(kernel, outs, flops, moved, specs, scratch=(), grant=12):
    return pl.pallas_call(
        kernel,
        out_shape=outs,
        in_specs=specs,
        out_specs=jax.tree.map(lambda _: VMEM, outs),
        scratch_shapes=scratch,
        compiler_params=pltpu.CompilerParams(vmem_limit_bytes=grant * 2**20),
        cost_estimate=pl.CostEstimate(flops=flops, bytes_accessed=moved, transcendentals=0),
    )


def regroup(piece):
    return [jnp.concatenate([piece(g, k) for g in range(G)], 1) for k in range(4)]


def prepare_kernel(count_ref, tiles_ref, hi_out, lo_out):
    for t in range(TR):
        count = count_ref[t]
        scale = 1.0 / jnp.sqrt(jnp.full((T, T), count, jnp.int32).astype(f32))
        for s in range(K):
            hi, lo = split(tiles_ref[t, s] * jnp.where(s < count, scale, 0.0))
            hi_out[t, :, T * s:T * s + T] = hi
            lo_out[t, :, T * s:T * s + T] = lo


def add_kernel(at, parts_ref, passed_ref, out_ref):
    for m in range(4):
        out_ref[m] = parts_ref[at + m] + passed_ref[m]


def near(pos_ref, col):
    return ((col // 4) % 4 - pos_ref[1] % 4 + 4) % 4, (col // 64 - pos_ref[0] + 2) % 2


def source_place(pos_ref, col):
    rel_q, rel_y = near(pos_ref, col)
    return rel_q * 8 + rel_y * 4 + (col // 16) % 4


def target_zh(z, rel_q, rel_y):
    by = jnp.where(rel_q == 3, -1, jnp.where(rel_q == 2, 2 - 4 * rel_y, rel_q))
    return (z + by + 16) % 16 // 4


def target_place(pos_ref, col):
    rel_q, rel_y = near(pos_ref, col)
    return rel_q * 8 + rel_y * 4 + ((col // 16) % 4 - target_zh(pos_ref[1], rel_q, rel_y) + 4) % 4


def gather_kernel(cols_ref, pos_ref, y0, y1, p0, p1, t0, t1, m0, m1, hi_ref, lo_ref, cot_ref, out_ref, held):
    for at, ref in enumerate((y0, y1, p0, p1, t0, t1, m0, m1)):
        for m in range(4):
            for t in range(TR):
                held[4 * at + m, t] = ref[m, :, T * t:T * t + T]
    for t in range(TR):
        picked = []
        for s in range(K):
            col = cols_ref[t, s]
            picked.append(held[source_place(pos_ref, col), col % 4])
        left_hi, left_lo = split(jnp.concatenate(picked, 1))
        both = dot(jnp.concatenate([left_hi, left_lo], 0), hi_ref[t], NT_DIMS)
        agg = both[:W] + both[W:] + dot(left_hi, lo_ref[t], NT_DIMS)
        parts = regroup(lambda g, k: agg[8 * g:8 * g + 8, W * k:W * k + W])
        cots = regroup(lambda g, k: cot_ref[8 * g:8 * g + 8, T * t + W * k:T * t + W * k + W])
        for k in range(4):
            out_ref[4 * t + k, 0:8, :] = parts[k]
            out_ref[4 * t + k, 8:16, :] = cots[k]


def node_rows(block):
    turned = block.reshape(T, T).T
    return jnp.concatenate([turned[W * g:W * g + W] for g in range(G)], 1)


def node_cols(rows):
    turned = jnp.concatenate([rows[:, T * g:T * g + T] for g in range(G)], 0)
    return turned.T.reshape(C, 8, T)


def weight_parts(w_ref):
    rows = [w_ref[c * W + g * 8:c * W + g * 8 + 8, :] for g in range(G) for c in range(C)]
    hi, lo = split(jnp.concatenate(rows, 0))
    old = lax.broadcasted_iota(jnp.int32, (F, F), 0)
    new = lax.broadcasted_iota(jnp.int32, (F, F), 1)
    source = ((new // 8) % C) * W + (new // (8 * C)) * 8 + new % 8
    order = jnp.where(old == source, 1.0, 0.0).astype(bf16)
    return dot(hi, order).astype(bf16), dot(lo, order).astype(bf16)


def layer_kernel(in_ref, w_ref, out_ref):
    w_hi, w_lo = weight_parts(w_ref)
    agg = node_rows(in_ref[:, 0:8, :])
    cot = node_rows(in_ref[:, 8:16, :])
    agg_hi, agg_lo = split(agg)
    both = dot(jnp.concatenate([agg_hi, agg_lo], 0), w_hi)
    pre = both[:W] + both[W:] + dot(agg_hi, w_lo)
    sig = jax.nn.sigmoid(pre)
    act = pre * sig
    grad = cot * (sig + act * (1.0 - sig))
    grad_hi, grad_lo = split(grad)
    both = dot(jnp.concatenate([grad_hi, grad_lo], 0), w_hi, NT_DIMS)
    back = both[:W] + both[W:] + dot(grad_hi, w_lo, NT_DIMS)
    out_ref[:, 0:8, :] = node_cols(back)
    out_ref[:, 8:16, :] = node_cols(act)
    left = jnp.concatenate([agg_hi, agg_lo, agg_hi], 0)
    right = jnp.concatenate([grad_hi, grad_hi, grad_lo], 0)
    for g in range(G):
        part = dot(left[:, T * g:T * g + T], right, TN_DIMS)
        for h in range(4):
            at = 16 + (4 * g + h) * 8
            out_ref[:, at:at + 8, :] = part[:, T * h:T * h + T].reshape(C, 8, T)


def spread_kernel(cols_ref, pos_ref, in_ref, hi_ref, lo_ref, act_ref, out_ref, weight_part):
    yh, z = pos_ref[0], pos_ref[1]
    total = in_ref[0, 16:16 + T, :]
    for c in range(1, C):
        total = total + in_ref[c, 16:16 + T, :]
    weight_part[...] = total.T
    out_ref[:, 0:TR * W, :] = jnp.zeros((32, TR * W, T), f32)
    for q in range(4):
        for y in range(2):
            for m in range(4):
                far = (m + target_zh(z, q, y)) % 4
                block = ((yh + y) % 2) * 16 + far * 4 + (z + q) % 4
                start = pl.multiple_of((block // 2) * 8, 8)
                out_ref[q * 8 + y * 4 + m, TR * W:BLK, :] = weight_part[pl.ds(start, 8), :]
    for t in range(TR):
        grad = regroup(lambda k, g: in_ref[4 * t + k, 0:8, W * g:W * g + W])
        act = regroup(lambda k, g: in_ref[4 * t + k, 8:16, W * g:W * g + W])
        act_ref[:, T * t:T * t + T] = jnp.concatenate(act, 0)
        grad_hi, grad_lo = split(jnp.concatenate(grad, 0))
        both = dot(jnp.concatenate([grad_hi, grad_lo], 0), hi_ref[t])
        sent = both[:W] + both[W:] + dot(grad_hi, lo_ref[t])
        for s in range(K):
            col = cols_ref[t, s]
            block = target_place(pos_ref, col)
            at = pl.ds(pl.multiple_of((col % 4) * W, W), W)
            out_ref[block, at, :] = out_ref[block, at, :] + sent[:, T * s:T * s + T]


def last_kernel(pos_ref, own_ref, up_ref, down_ref, grad_ref, weight_ref):
    total = own_ref[...] + up_ref[...] + down_ref[...]
    for t in range(TR):
        grad_ref[:, T * t:T * t + T] = total[W * t:W * t + W]
    piece = total[TR * W:BLK]
    odd = jnp.concatenate([piece[:, 16:], piece[:, :16]], 1)
    piece = jnp.where(pos_ref[1] % 2 == 1, odd, piece)
    for h in range(2):
        cut = [piece[:, W * g + 8 * h:W * g + 8 * h + 8] for g in range(G)]
        weight_ref[8 * h:8 * h + 8, :] = jnp.concatenate(cut, 1)


def shift(size, by):
    return [(i, (i + by) % size) for i in range(size)]


def along(x, by):
    return lax.ppermute(x, RING, shift(16, by))


def across(x):
    return lax.ppermute(x, "yh", shift(2, 1))


def local(features, weight, tile_cols, tile_count, tile_values, cotangent):
    pos = jnp.stack([lax.axis_index("yh"), lax.axis_index(RING)]).astype(jnp.int32)
    shape = jax.ShapeDtypeStruct

    with jax.named_scope("gather_features"):
        far = lax.all_gather(features.T, "zh")
        other = across(far)
        m0, p0 = along(far, 1), along(far, -1)
        p1, m1 = along(other, -1), along(other, 1)
        t0, t1 = along(m0, 1), along(p1, -1)
    tiles_hi, tiles_lo = call(
        prepare_kernel, (shape((TR, T, K * T), bf16), shape((TR, T, K * T), bf16)), 10**7, 6 * 2**20, [SMEM, VMEM],
    )(tile_count, tile_values)
    packed = call(
        gather_kernel, shape((C, 16, T), f32), 10**8, 6 * 2**20, [SMEM] * 2 + [VMEM] * 11,
        [pltpu.VMEM((32, TR, W, T), f32)],
    )(tile_cols, pos, far, other, p0, p1, t0, t1, m0, m1, tiles_hi, tiles_lo, cotangent.T)
    with jax.named_scope("to_nodes"):
        packed = lax.all_to_all(packed, COLS, 0, 0)
    layer = call(layer_kernel, shape((C, 16 + T, T), f32), 10**8, 3 * 2**20, [VMEM] * 2)(packed, weight)
    with jax.named_scope("to_features"):
        layer = lax.all_to_all(layer, COLS, 0, 0)
    activated, parts = call(
        spread_kernel, (shape((W, TR * T), f32), shape((32, BLK, T), f32)), 10**8, 7 * 2**20,
        [SMEM] * 2 + [VMEM] * 3, [pltpu.VMEM((T, T), f32)],
    )(tile_cols, pos, layer, tiles_hi, tiles_lo)
    with jax.named_scope("add_blocks"):
        flat, parts = parts, parts.reshape(4, 2, 4, BLK, T)
        t1, t0 = along(parts[2, 1], -1), along(parts[2, 0], 1)
        m1 = along(parts[1, 1], 1)
        add = lambda at, passed: call(
            functools.partial(add_kernel, at), shape((4, BLK, T), f32), 10**5, 2**20, [VMEM] * 2, grant=4
        )(flat, passed)
        p1 = along(add(28, t1), -1)
        p0, m0 = along(parts[3, 0], -1), along(add(8, t0), 1)
        y1 = across(parts[0, 1] + m1 + p1)
        y0 = parts[0, 0] + m0 + p0 + y1
        down = along(y0[3], -4)
        up = along(y0[1] + along(y0[2], 4), 4)
    grad_features, grad_weight = call(
        last_kernel, (shape((W, TR * T), f32), shape((16, W), f32)), 10**6, 2**19, [SMEM] + [VMEM] * 3,
    )(pos, y0[0], up, down)
    return activated.T, grad_features.T, grad_weight.T


def solution(mesh):
    grid = Mesh(mesh.devices.reshape(2, 4, 4, 2, 4, 2), ROWS + COLS)
    return jax.shard_map(
        local,
        mesh=grid,
        in_specs=(P(ROWS, COLS), P(), P(ROWS, None), P(ROWS), P(ROWS, None, None, None), P(ROWS, COLS)),
        out_specs=(P(ROWS, COLS), P(ROWS, COLS), P(COLS, ROWS)),
        check_vma=False,
    )
```

```python
import functools

import jax
import jax.numpy as jnp
from jax import lax
from jax.experimental import pallas as pl
from jax.experimental.pallas import tpu as pltpu
from jax.sharding import Mesh, PartitionSpec as P

ROWS = ("yh", "zh", "zl")
RING = ("zh", "zl")
COLS = ("yl", "x", "core")
F = 512
W = 32
T = 128
K = 12
TR = 4
C = 16
G = 4
BLK = TR * W + 8
f32, bf16 = jnp.float32, jnp.bfloat16
VMEM = pl.BlockSpec(memory_space=pltpu.VMEM)
SMEM = pl.BlockSpec(memory_space=pltpu.SMEM)
NT_DIMS = (((1,), (1,)), ((), ()))
NN_DIMS = (((1,), (0,)), ((), ()))
TN_DIMS = (((0,), (0,)), ((), ()))


def dot(a, b, dims=NN_DIMS):
    return lax.dot_general(a, b, dims, preferred_element_type=f32)


def split(x):
    hi = x.astype(bf16)
    return hi, (x - hi.astype(f32)).astype(bf16)


def call(kernel, outs, flops, moved, specs, scratch=(), grant=12):
    return pl.pallas_call(
        kernel,
        out_shape=outs,
        in_specs=specs,
        out_specs=jax.tree.map(lambda _: VMEM, outs),
        scratch_shapes=scratch,
        compiler_params=pltpu.CompilerParams(vmem_limit_bytes=grant * 2**20),
        cost_estimate=pl.CostEstimate(flops=flops, bytes_accessed=moved, transcendentals=0),
    )


def regroup(piece):
    return [jnp.concatenate([piece(g, k) for g in range(G)], 1) for k in range(4)]


def prepare_kernel(count_ref, w_ref, tiles_ref, w_out, hi_out, lo_out):
    for t in range(TR):
        count = count_ref[t]
        scale = 1.0 / jnp.sqrt(jnp.full((T, T), count, jnp.int32).astype(f32))
        for s in range(K):
            hi, lo = split(tiles_ref[t, s] * jnp.where(s < count, scale, 0.0))
            hi_out[t, :, T * s:T * s + T] = hi
            lo_out[t, :, T * s:T * s + T] = lo
    rows = [w_ref[c * W + g * 8:c * W + g * 8 + 8, :] for g in range(G) for c in range(C)]
    hi, lo = split(jnp.concatenate(rows, 0))
    old = lax.broadcasted_iota(jnp.int32, (F, F), 0)
    new = lax.broadcasted_iota(jnp.int32, (F, F), 1)
    source = ((new // 8) % C) * W + (new // (8 * C)) * 8 + new % 8
    order = jnp.where(old == source, 1.0, 0.0).astype(bf16)
    w_out[0] = dot(hi, order).astype(bf16)
    w_out[1] = dot(lo, order).astype(bf16)


def add_kernel(at, parts_ref, passed_ref, out_ref):
    for m in range(4):
        out_ref[m] = parts_ref[at + m] + passed_ref[m]


def near(pos_ref, col):
    return ((col // 4) % 4 - pos_ref[1] % 4 + 4) % 4, (col // 64 - pos_ref[0] + 2) % 2


def source_place(pos_ref, col):
    rel_q, rel_y = near(pos_ref, col)
    return rel_q * 8 + rel_y * 4 + (col // 16) % 4


def target_zh(z, rel_q, rel_y):
    by = jnp.where(rel_q == 3, -1, jnp.where(rel_q == 2, 2 - 4 * rel_y, rel_q))
    return (z + by + 16) % 16 // 4


def target_place(pos_ref, col):
    rel_q, rel_y = near(pos_ref, col)
    return rel_q * 8 + rel_y * 4 + ((col // 16) % 4 - target_zh(pos_ref[1], rel_q, rel_y) + 4) % 4


def gather_kernel(cols_ref, pos_ref, y0, y1, p0, p1, t0, t1, m0, m1, hi_ref, lo_ref, cot_ref, out_ref, held):
    for at, ref in enumerate((y0, y1, p0, p1, t0, t1, m0, m1)):
        for m in range(4):
            for t in range(TR):
                held[4 * at + m, t] = ref[m, :, T * t:T * t + T]
    for t in range(TR):
        picked = []
        for s in range(K):
            col = cols_ref[t, s]
            picked.append(held[source_place(pos_ref, col), col % 4])
        left_hi, left_lo = split(jnp.concatenate(picked, 1))
        both = dot(jnp.concatenate([left_hi, left_lo], 0), hi_ref[t], NT_DIMS)
        agg = both[:W] + both[W:] + dot(left_hi, lo_ref[t], NT_DIMS)
        parts = regroup(lambda g, k: agg[8 * g:8 * g + 8, W * k:W * k + W])
        cots = regroup(lambda g, k: cot_ref[8 * g:8 * g + 8, T * t + W * k:T * t + W * k + W])
        for k in range(4):
            out_ref[4 * t + k, 0:8, :] = parts[k]
            out_ref[4 * t + k, 8:16, :] = cots[k]


def node_rows(block):
    turned = block.reshape(T, T).T
    return jnp.concatenate([turned[W * g:W * g + W] for g in range(G)], 1)


def node_cols(rows):
    turned = jnp.concatenate([rows[:, T * g:T * g + T] for g in range(G)], 0)
    return turned.T.reshape(C, 8, T)


def layer_kernel(in_ref, w_ref, out_ref):
    agg = node_rows(in_ref[:, 0:8, :])
    cot = node_rows(in_ref[:, 8:16, :])
    agg_hi, agg_lo = split(agg)
    both = dot(jnp.concatenate([agg_hi, agg_lo], 0), w_ref[0])
    pre = both[:W] + both[W:] + dot(agg_hi, w_ref[1])
    sig = jax.nn.sigmoid(pre)
    act = pre * sig
    grad = cot * (sig + act * (1.0 - sig))
    grad_hi, grad_lo = split(grad)
    both = dot(jnp.concatenate([grad_hi, grad_lo], 0), w_ref[0], NT_DIMS)
    back = both[:W] + both[W:] + dot(grad_hi, w_ref[1], NT_DIMS)
    out_ref[:, 0:8, :] = node_cols(back)
    out_ref[:, 8:16, :] = node_cols(act)
    left = jnp.concatenate([agg_hi, agg_lo, agg_hi], 0)
    right = jnp.concatenate([grad_hi, grad_hi, grad_lo], 0)
    for g in range(G):
        part = dot(left[:, T * g:T * g + T], right, TN_DIMS)
        for h in range(4):
            at = 16 + (4 * g + h) * 8
            out_ref[:, at:at + 8, :] = part[:, T * h:T * h + T].reshape(C, 8, T)


def spread_kernel(cols_ref, pos_ref, in_ref, hi_ref, lo_ref, act_ref, out_ref, weight_part):
    yh, z = pos_ref[0], pos_ref[1]
    total = in_ref[0, 16:16 + T, :]
    for c in range(1, C):
        total = total + in_ref[c, 16:16 + T, :]
    weight_part[...] = total.T
    out_ref[:, 0:TR * W, :] = jnp.zeros((32, TR * W, T), f32)
    for q in range(4):
        for y in range(2):
            for m in range(4):
                far = (m + target_zh(z, q, y)) % 4
                block = ((yh + y) % 2) * 16 + far * 4 + (z + q) % 4
                start = pl.multiple_of((block // 2) * 8, 8)
                out_ref[q * 8 + y * 4 + m, TR * W:BLK, :] = weight_part[pl.ds(start, 8), :]
    for t in range(TR):
        grad = regroup(lambda k, g: in_ref[4 * t + k, 0:8, W * g:W * g + W])
        act = regroup(lambda k, g: in_ref[4 * t + k, 8:16, W * g:W * g + W])
        act_ref[:, T * t:T * t + T] = jnp.concatenate(act, 0)
        grad_hi, grad_lo = split(jnp.concatenate(grad, 0))
        upper = jnp.concatenate([grad_hi, grad_hi], 1)
        lower = jnp.concatenate([grad_lo, jnp.zeros_like(grad_lo)], 1)
        both = dot(jnp.concatenate([upper, lower], 0), jnp.concatenate([hi_ref[t], lo_ref[t]], 0))
        sent = both[:W] + both[W:]
        for s in range(K):
            col = cols_ref[t, s]
            block = target_place(pos_ref, col)
            at = pl.ds(pl.multiple_of((col % 4) * W, W), W)
            out_ref[block, at, :] = out_ref[block, at, :] + sent[:, T * s:T * s + T]


def last_kernel(pos_ref, own_ref, up_ref, down_ref, grad_ref, weight_ref):
    total = own_ref[...] + up_ref[...] + down_ref[...]
    for t in range(TR):
        grad_ref[:, T * t:T * t + T] = total[W * t:W * t + W]
    piece = total[TR * W:BLK]
    odd = jnp.concatenate([piece[:, 16:], piece[:, :16]], 1)
    piece = jnp.where(pos_ref[1] % 2 == 1, odd, piece)
    for h in range(2):
        cut = [piece[:, W * g + 8 * h:W * g + 8 * h + 8] for g in range(G)]
        weight_ref[8 * h:8 * h + 8, :] = jnp.concatenate(cut, 1)


def shift(size, by):
    return [(i, (i + by) % size) for i in range(size)]


def along(x, by):
    return lax.ppermute(x, RING, shift(16, by))


def across(x):
    return lax.ppermute(x, "yh", shift(2, 1))


def local(features, weight, tile_cols, tile_count, tile_values, cotangent):
    pos = jnp.stack([lax.axis_index("yh"), lax.axis_index(RING)]).astype(jnp.int32)
    shape = jax.ShapeDtypeStruct

    with jax.named_scope("gather_features"):
        far = lax.all_gather(features.T, "zh")
        other = across(far)
        m0, p0 = along(far, 1), along(far, -1)
        p1, m1 = along(other, -1), along(other, 1)
        t0, t1 = along(m0, 1), along(p1, -1)
    weight_parts, tiles_hi, tiles_lo = call(
        prepare_kernel,
        (shape((2, F, F), bf16), shape((TR, T, K * T), bf16), shape((TR, T, K * T), bf16)),
        4 * F**3, 8 * 2**20, [SMEM, VMEM, VMEM],
    )(tile_count, weight, tile_values)
    packed = call(
        gather_kernel, shape((C, 16, T), f32), 10**8, 6 * 2**20, [SMEM] * 2 + [VMEM] * 11,
        [pltpu.VMEM((32, TR, W, T), f32)],
    )(tile_cols, pos, far, other, p0, p1, t0, t1, m0, m1, tiles_hi, tiles_lo, cotangent.T)
    with jax.named_scope("to_nodes"):
        packed = lax.all_to_all(packed, COLS, 0, 0)
    layer = call(layer_kernel, shape((C, 16 + T, T), f32), 10**8, 3 * 2**20, [VMEM] * 2)(packed, weight_parts)
    with jax.named_scope("to_features"):
        layer = lax.all_to_all(layer, COLS, 0, 0)
    activated, parts = call(
        spread_kernel, (shape((W, TR * T), f32), shape((32, BLK, T), f32)), 10**8, 7 * 2**20,
        [SMEM] * 2 + [VMEM] * 3, [pltpu.VMEM((T, T), f32)],
    )(tile_cols, pos, layer, tiles_hi, tiles_lo)
    with jax.named_scope("add_blocks"):
        flat, parts = parts, parts.reshape(4, 2, 4, BLK, T)
        t1, t0 = along(parts[2, 1], -1), along(parts[2, 0], 1)
        m1 = along(parts[1, 1], 1)
        add = lambda at, passed: call(
            functools.partial(add_kernel, at), shape((4, BLK, T), f32), 10**5, 2**20, [VMEM] * 2, grant=4
        )(flat, passed)
        p1 = along(add(28, t1), -1)
        p0, m0 = along(parts[3, 0], -1), along(add(8, t0), 1)
        y1 = across(parts[0, 1] + m1 + p1)
        y0 = parts[0, 0] + m0 + p0 + y1
        down = along(y0[3], -4)
        up = along(y0[1] + along(y0[2], 4), 4)
    grad_features, grad_weight = call(
        last_kernel, (shape((W, TR * T), f32), shape((16, W), f32)), 10**6, 2**19, [SMEM] + [VMEM] * 3,
    )(pos, y0[0], up, down)
    return activated.T, grad_features.T, grad_weight.T


def solution(mesh):
    grid = Mesh(mesh.devices.reshape(2, 4, 4, 2, 4, 2), ROWS + COLS)
    return jax.shard_map(
        local,
        mesh=grid,
        in_specs=(P(ROWS, COLS), P(), P(ROWS, None), P(ROWS), P(ROWS, None, None, None), P(ROWS, COLS)),
        out_specs=(P(ROWS, COLS), P(ROWS, COLS), P(COLS, ROWS)),
        check_vma=False,
    )
```
